32 devices in a mesh: item: 4 (over y, x), seq: 8 (over z, core).
Axes of the slice: x: 2, y: 2, z: 4, core: 2. Of those that a mesh axis runs over, the one named last changes fastest.
Arguments:
- inputs: float32 [4, 2048, 768], P('item', 'seq'), may hold values from -6 to 6
- lengths: int32 [4], P('item'), may hold values from 512 to 2048, as said below
- pad_mask: int32 [4, 2048], P('item', 'seq'), may hold values 0 or 1
- hash_proj: float32 [64, 256], replicated, may hold values from -6 to 6
- w_query: bfloat16 [768, 768], replicated, may hold values from -0.21875 to 0.21875
- b_query: float32 [768], replicated, may hold values from -1.75 to 1.75
- w_key: bfloat16 [768, 768], replicated, may hold values from -0.21875 to 0.21875
- b_key: float32 [768], replicated, may hold values from -1.75 to 1.75
- w_value: bfloat16 [768, 768], replicated, may hold values from -0.21875 to 0.21875
- b_value: float32 [768], replicated, may hold values from -1.75 to 1.75
- conv_taps: float32 [12, 9], replicated, may hold values from -0.875 to 0.875
- w_out: bfloat16 [768, 768], replicated, may hold values from -0.625 to 0.625
- b_out: float32 [768], replicated, may hold values from -1.75 to 1.75
- gain_one: float32 [768], replicated, may hold values from 0.5 to 1.5
- bias_one: float32 [768], replicated, may hold values from -1.75 to 1.75
- w_up: bfloat16 [768, 3072], replicated, may hold values from -0.21875 to 0.21875
- b_up: float32 [3072], replicated, may hold values from -1.75 to 1.75
- w_down: bfloat16 [3072, 768], replicated, may hold values from -0.109375 to 0.109375
- b_down: float32 [768], replicated, may hold values from -1.75 to 1.75
- gain_two: float32 [768], replicated, may hold values from 0.5 to 1.5
- bias_two: float32 [768], replicated, may hold values from -1.75 to 1.75
- out_grad: float32 [4, 2048, 768], P('item', 'seq'), may hold values from -6 to 6
Outputs:
- output: float32 [4, 2048, 768], P('item', 'seq')
- d_inputs: float32 [4, 2048, 768], P('item', 'seq')
- counts: float32 [4, 12, 32, 256], P('item', None, 'seq')
- d_w_query: float32 [768, 768], replicated
- d_b_query: float32 [768], replicated
- d_w_key: float32 [768, 768], replicated
- d_b_key: float32 [768], replicated
- d_w_value: float32 [768, 768], replicated
- d_b_value: float32 [768], replicated
- d_conv_taps: float32 [12, 9], replicated
- d_w_out: float32 [768, 768], replicated
- d_b_out: float32 [768], replicated
- d_gain_one: float32 [768], replicated
- d_bias_one: float32 [768], replicated
- d_w_up: float32 [768, 3072], replicated
- d_b_up: float32 [3072], replicated
- d_w_down: float32 [3072, 768], replicated
- d_b_down: float32 [768], replicated
- d_gain_two: float32 [768], replicated
- d_bias_two: float32 [768], replicated
The draws below stay inside these ranges and needn't reach their ends.
Inputs may be any that keep to these rules, and one draw needn't show every extreme that they name: `lengths`: one item, drawn from the seed, has length 2048; every other item has at least 512 tokens.
All inputs are finite; a program needn't handle non-finite values. No bound on the sum of `pad_mask` on one device may be relied on, other than what follows from the above.
Results may differ from the reference program's by a relative error of at most 0.0003.
Values sent between devices are 32-bit elements; how exact they have to be, the bound alone decides.
No kernel may reach another device: no remote copies, remote signals or barrier semaphores. Data moves between devices by JAX's collectives and lax.ppermute only.
A program may use at most 256 MiB of HBM per device.

```python
import jax
import jax.numpy as jnp
from jax import lax

MODEL_WIDTH = 768
FF = 3072
HEAD_COUNT = 12
HEAD_SIZE = 64
HASH_COUNT = 32
HASH_BITS = 8
CONV = 9
SEQ_LEN = 2048
ITEMS = 4


def draw_lengths(key, part):
    picks = jax.random.randint(jax.random.fold_in(key, 11), (ITEMS,), SEQ_LEN // 4, SEQ_LEN + 1)
    chosen = jax.random.randint(jax.random.fold_in(key, 12), (), 0, ITEMS)
    return jnp.where(jnp.arange(ITEMS) == chosen, SEQ_LEN, picks).astype(jnp.int32)


def set_ends(array, key, smallest, high):
    longest = array.shape.index(max(array.shape))
    spots = []
    for shift in (0, 1):
        where = [jax.random.randint(jax.random.fold_in(key, axis), (), 0, length) for axis, length in enumerate(array.shape)]
        where[longest] = (where[longest] + shift) % array.shape[longest]
        spots.append(tuple(where))
    return array.at[spots[0]].set(smallest).at[spots[1]].set(high)


def level_of(stream_key, extent, cuts, least, largest):
    level = 1.0
    for dim, shards_of in cuts:
        steps = jax.random.uniform(jax.random.fold_in(jax.random.fold_in(stream_key, 6), dim), (shards_of,), jnp.float32, least / len(cuts), largest / len(cuts))
        level = level * jnp.repeat(jnp.exp(steps), extent[dim] // shards_of).reshape((-1,) + (1,) * (len(extent) - 1 - dim))
    return level


def noise(own_key, dims, scale, limit, split=(), held_as=jnp.bfloat16):
    factor_of = level_of(own_key, dims, split, -0.22, 0.18) if split else 1.0
    result = jax.random.normal(own_key, dims, jnp.float32) * scale * factor_of
    return jnp.minimum(jnp.maximum(result, -limit), limit).astype(held_as)


def setup_inputs(seed: int = 0) -> dict:
    streams_of = jax.random.split(jax.random.key(seed), 23)
    return {
        "inputs": noise(streams_of[0], (ITEMS, SEQ_LEN, MODEL_WIDTH), 1.0, 6.0, ((0, 4), (1, 8)), jnp.float32),
        "lengths": draw_lengths(jax.random.fold_in(streams_of[22], 71), 0),
        "pad_mask": set_ends((jax.random.randint(streams_of[2], (ITEMS, SEQ_LEN), 0, 8) < 7).astype(jnp.int32), jax.random.fold_in(streams_of[2], 1), 0, 1),
        "hash_proj": noise(streams_of[3], (HEAD_SIZE, HASH_COUNT * HASH_BITS), 1.0, 6.0, (), jnp.float32),
        "w_query": noise(streams_of[4], (MODEL_WIDTH, MODEL_WIDTH), MODEL_WIDTH ** -0.5, 0.21875),
        "b_query": noise(streams_of[5], (MODEL_WIDTH,), 0.3, 1.75, (), jnp.float32),
        "w_key": noise(streams_of[6], (MODEL_WIDTH, MODEL_WIDTH), MODEL_WIDTH ** -0.5, 0.21875),
        "b_key": noise(streams_of[7], (MODEL_WIDTH,), 0.3, 1.75, (), jnp.float32),
        "w_value": noise(streams_of[8], (MODEL_WIDTH, MODEL_WIDTH), MODEL_WIDTH ** -0.5, 0.21875),
        "b_value": noise(streams_of[9], (MODEL_WIDTH,), 0.3, 1.75, (), jnp.float32),
        "conv_taps": noise(streams_of[10], (HEAD_COUNT, CONV), 0.15, 0.875, (), jnp.float32),
        "w_out": noise(streams_of[11], (MODEL_WIDTH, MODEL_WIDTH), (MODEL_WIDTH // 8) ** -0.5, 0.625),
        "b_out": noise(streams_of[12], (MODEL_WIDTH,), 0.3, 1.75, (), jnp.float32),
        "gain_one": jnp.clip(1.0 + 0.1 * jax.random.normal(streams_of[13], (MODEL_WIDTH,), jnp.float32), 0.5, 1.5),
        "bias_one": noise(streams_of[14], (MODEL_WIDTH,), 0.3, 1.75, (), jnp.float32),
        "w_up": noise(streams_of[15], (MODEL_WIDTH, FF), MODEL_WIDTH ** -0.5, 0.21875),
        "b_up": noise(streams_of[16], (FF,), 0.3, 1.75, (), jnp.float32),
        "w_down": noise(streams_of[17], (FF, MODEL_WIDTH), FF ** -0.5, 0.109375),
        "b_down": noise(streams_of[18], (MODEL_WIDTH,), 0.3, 1.75, (), jnp.float32),
        "gain_two": jnp.clip(1.0 + 0.1 * jax.random.normal(streams_of[19], (MODEL_WIDTH,), jnp.float32), 0.5, 1.5),
        "bias_two": noise(streams_of[20], (MODEL_WIDTH,), 0.3, 1.75, (), jnp.float32),
        "out_grad": noise(streams_of[21], (ITEMS, SEQ_LEN, MODEL_WIDTH), 1.0, 6.0, ((0, 4), (1, 8)), jnp.float32),
    }


highest = lax.Precision.HIGHEST
softness_scale = 2.0

def unit_rows(matrix):
    return matrix * lax.rsqrt(lax.optimization_barrier(jnp.mean(matrix * matrix, axis=-1, keepdims=True)) + 1e-06) * 0.125

def hash_signs(matrix, hash_proj):
    sequence_length = matrix.shape[0]
    normed = unit_rows(matrix.reshape(sequence_length, HEAD_COUNT, HEAD_SIZE))
    rotation_angles = jnp.einsum('thd,dk->htk', normed, hash_proj, precision=highest)
    return jnp.tanh(softness_scale * rotation_angles).reshape(HEAD_COUNT, sequence_length, HASH_COUNT, HASH_BITS).transpose(0, 2, 3, 1)

def member(signs):
    groups = signs.shape[0]
    sequence_length = signs.shape[2]
    weights = jnp.ones((groups, 1, sequence_length), jnp.float32)
    for column in range(signs.shape[1]):
        upper = 0.5 * (1.0 + signs[:, column])
        lower = 0.5 * (1.0 - signs[:, column])
        weights = jnp.stack([weights * upper[:, None], weights * lower[:, None]], axis=2)
        weights = weights.reshape(groups, -1, sequence_length)
    return weights

def fill(key_signs, valid_mask, value_rows):
    weights = member(key_signs) * valid_mask
    tables = jnp.einsum('gbt,td->gbd', weights, value_rows, precision=highest)
    return (tables, lax.optimization_barrier(jnp.sum(weights, axis=2)))

def read(query_signs, tables, counts):
    weights = member(query_signs)
    numer = jnp.einsum('gbt,gbd->td', weights, tables, precision=highest)
    denom = jnp.einsum('gbt,gb->t', weights, counts, precision=highest)
    return (numer, denom)

def layer_norm(matrix):
    centered = matrix - lax.optimization_barrier(jnp.mean(matrix, axis=-1, keepdims=True))
    return centered * lax.rsqrt(lax.optimization_barrier(jnp.mean(centered * centered, axis=-1, keepdims=True)) + 1e-05)

def project(hidden_in, w_query, b_query, w_key, b_key, w_value, b_value):
    query = jnp.dot(hidden_in, w_query, precision=highest) + b_query
    keys = jnp.dot(hidden_in, w_key, precision=highest) + b_key
    value_rows = jnp.dot(hidden_in, w_value, precision=highest) + b_value
    return (query, keys, value_rows)

def post(attn, hidden_in, w_out, b_out, gain_one, bias_one, w_up, b_up, w_down, b_down, gain_two, bias_two):
    first = layer_norm(hidden_in + jnp.dot(attn, w_out, precision=highest) + b_out) * gain_one + bias_one
    inner = jax.nn.gelu(jnp.dot(first, w_up, precision=highest) + b_up, approximate=False)
    second = first + jnp.dot(inner, w_down, precision=highest) + b_down
    return layer_norm(second) * gain_two + bias_two

def forward(hidden_in, params, hash_proj, valid_mask):
    sequence_length = hidden_in.shape[0]
    query, keys, value_rows = project(hidden_in, *params[:6])
    masked_values = value_rows * valid_mask[:, None]
    q_signs = hash_signs(query, hash_proj)
    k_signs = hash_signs(keys, hash_proj)
    per_head_values = masked_values.reshape(sequence_length, HEAD_COUNT, HEAD_SIZE).transpose(1, 0, 2)

    def one_head(packed):
        tables, counts = fill(packed[1], valid_mask, packed[2])
        numer, denom = read(packed[0], tables, counts)
        return (numer, denom, counts)
    numer, denom, counts = lax.map(jax.checkpoint(one_head), (q_signs, k_signs, per_head_values))
    denom = denom.T + HASH_COUNT
    mixed = (numer.transpose(1, 0, 2) / denom[:, :, None]).reshape(sequence_length, MODEL_WIDTH)
    window_half = CONV // 2
    padded_rows = jnp.pad(masked_values, ((window_half, window_half), (0, 0)))
    bucket_spread = jnp.repeat(params[6], HEAD_SIZE, axis=0)
    conv = jnp.zeros((sequence_length, MODEL_WIDTH), jnp.float32)
    for shift_amount in range(CONV):
        conv = conv + padded_rows[shift_amount:shift_amount + sequence_length] * bucket_spread[:, shift_amount]
    output = post(mixed + conv, hidden_in, *params[7:])
    return (output, counts)

def reference(inputs, lengths, pad_mask, hash_proj, w_query, b_query, w_key, b_key, w_value, b_value, conv_taps, w_out, b_out, gain_one, bias_one, w_up, b_up, w_down, b_down, gain_two, bias_two, out_grad):
    params = tuple((param.astype(jnp.float32) for param in (w_query, b_query, w_key, b_key, w_value, b_value, conv_taps, w_out, b_out, gain_one, bias_one, w_up, b_up, w_down, b_down, gain_two, bias_two)))
    sequence_length = inputs.shape[1]
    position = lax.iota(jnp.int32, sequence_length)

    def one_item(totals, packed):
        hidden_in, item_len, item_mask, cotangent = packed
        valid_mask = ((position < item_len) & (item_mask == 1)).astype(jnp.float32)

        def whole(hidden_arg, *param_args):
            return forward(hidden_arg, param_args, hash_proj, valid_mask)
        output, pull, counts = jax.vjp(whole, hidden_in, *params, has_aux=True)
        grads = pull(cotangent)
        totals = tuple((total + grad for total, grad in zip(totals, grads[1:])))
        return (totals, (output, grads[0], counts))
    start = tuple((jnp.zeros(param.shape, jnp.float32) for param in params))
    totals, (outputs, d_inputs, counts) = lax.scan(one_item, start, (inputs, lengths, pad_mask, out_grad))
    return (outputs, d_inputs, counts, *totals)
```

```python
import functools
import math

import jax
import jax.numpy as jnp
from jax import lax
from jax.experimental import pallas as pl
from jax.experimental.pallas import tpu as pltpu
from jax.sharding import PartitionSpec as P

MODEL_WIDTH = 768
HEAD_COUNT = 12
HEAD_SIZE = 64
HASH_COUNT = 32
HASH_BITS = 8
BUCKETS = 256
CONV = 9
HALF = CONV // 2
ROWS = 80
CHUNK = 256
VMEM_BYTES = 56 * 1024 * 1024

BF = jnp.bfloat16
F32 = jnp.float32


def split(x):
    hi = x.astype(BF)
    return hi, (x - hi.astype(F32)).astype(BF)


def parts_of(x):
    hi = lax.reduce_precision(x, 8, 7)
    return hi.astype(BF), (x - hi).astype(BF)


def dot(a, b):
    return jnp.dot(a, b, preferred_element_type=F32)


def dot3(a, b):
    ah, al = split(a)
    bh, bl = split(b)
    return dot(ah, bh) + dot(ah, bl) + dot(al, bh)


def contract(a, b, i, j):
    return lax.dot_general(a, b, (((i,), (j,)), ((), ())), preferred_element_type=F32)


def by_weight(x, w, i, j):
    hi, lo = parts_of(x)
    return contract(hi, w, i, j) + contract(lo, w, i, j)


def outer_sum(a, b):
    ah, al = parts_of(a)
    bh, bl = parts_of(b)
    return contract(
        jnp.concatenate([ah, al, ah], axis=0), jnp.concatenate([bh, bh, bl], axis=0), 0, 0
    )


def factors(s8):
    w = s8.shape[1]
    r = lax.broadcasted_iota(jnp.int32, (8, w), 0)
    rows = [jnp.broadcast_to(s8[j : j + 1], (8, w)) for j in range(8)]
    low = [jnp.where((r & m) != 0, rows[j], 1.0) for j, m in ((5, 4), (6, 2), (7, 1))]
    return r, rows, low


def monomials(rows, low):
    out = [low[0] * low[1] * low[2]]
    for j in (4, 3, 2, 1, 0):
        out = out + [rows[j] * x for x in out]
    return out


def row_sums(r, parts):
    step = 1
    while len(parts) > 1:
        bit = (r & step) != 0
        parts = [
            jnp.where(bit, b, a) + pltpu.roll(jnp.where(bit, a, b), step, 0)
            for a, b in zip(parts[0::2], parts[1::2])
        ]
        step *= 2
    return parts[0]


def sign_grad(r, rows, low, phi, d):
    c = [d[8 * v : 8 * v + 8] for v in range(32)]
    parts = []
    for j in range(5):
        half = len(c) // 2
        acc = phi[0] * c[half]
        for n in range(1, half):
            acc = acc + phi[n] * c[half + n]
        parts.append(acc)
        c = [c[n] + rows[j] * c[half + n] for n in range(half)]
    m = c[0]
    zero = jnp.zeros_like(m)
    parts.append(jnp.where((r & 4) != 0, m * low[1] * low[2], zero))
    parts.append(jnp.where((r & 2) != 0, m * low[0] * low[2], zero))
    parts.append(jnp.where((r & 1) != 0, m * low[0] * low[1], zero))
    return row_sums(r, parts)


def norm_scale(u):
    return lax.rsqrt(jnp.mean(u * u, axis=0, keepdims=True) + 1e-06)


def signs_of(u, proj):
    return jnp.tanh(2.0 * dot3(proj, u * (norm_scale(u) * 0.125)))


def columns(rows64, row):
    t = jnp.concatenate([rows64, row, jnp.zeros((63, row.shape[1]), F32)], axis=0).T
    return jnp.concatenate(split(t), axis=1)


def stacked(rows64, row):
    width = row.shape[1]
    hi, lo = split(jnp.concatenate([rows64, row, jnp.zeros((15, width), F32)], axis=0))
    return jnp.concatenate([hi, hi, lo, jnp.zeros((16, width), BF)], axis=0)


def beside(tab):
    hi = tab.astype(BF).astype(F32)
    lo = pltpu.roll(tab - hi, ROWS, 1)
    again = pltpu.roll(hi, 2 * ROWS - 128, 1)
    lane = lax.broadcasted_iota(jnp.int32, tab.shape, 1)
    return jnp.concatenate(
        [jnp.where(lane < ROWS, hi, lo), jnp.where(lane < 2 * ROWS - 128, lo, again)], axis=1
    ).astype(BF)


def halves(tab):
    return jnp.concatenate(split(tab.T[:ROWS]), axis=0)


def shifted(x, offset):
    if offset == 0:
        return x
    width = x.shape[1]
    t = lax.broadcasted_iota(jnp.int32, x.shape, 1) + offset
    return jnp.where((t >= 0) & (t < width), pltpu.roll(x, (-offset) % width, 1), 0.0)


def reorder(x, outer, inner, block):
    return jnp.concatenate(
        [
            x[:, (o * inner + i) * block : (o * inner + i + 1) * block]
            for i in range(inner)
            for o in range(outer)
        ],
        axis=1,
    )


def fwd_kernel(
    hashes, groups, inner, q_ref, k_ref, v_ref, valid_ref, proj_ref, taps_ref,
    num_ref, tab_ref, conv_ref, sq, sk, cols,
):
    head = pl.program_id(0)
    width = q_ref.shape[2]
    block = width // (groups * inner)
    sq[...] = signs_of(q_ref[0], proj_ref[...])
    sk[...] = signs_of(k_ref[0], proj_ref[...])
    v = v_ref[0]
    cols[...] = columns(v, valid_ref[...])
    num_ref[0] = jnp.zeros(num_ref.shape[1:], F32)
    natural = reorder(v, inner, groups, block)
    conv = jnp.zeros(natural.shape, F32)
    for j in range(CONV):
        conv = conv + shifted(natural, j - HALF) * taps_ref[head, j]
    conv_ref[0] = reorder(conv, groups, inner, block)

    @pl.loop(0, hashes)
    def _(g):
        base = pl.multiple_of(g * 8, 8)
        acc = None
        for c in range(0, width, CHUNK):
            _, rows, low = factors(sk[pl.ds(base, 8), c : c + CHUNK])
            hi, lo = split(jnp.concatenate(monomials(rows, low), axis=0))
            value = cols[c : c + CHUNK, :]
            p = dot(hi, value) + dot(lo, value)
            acc = p if acc is None else acc + p
        tab = (acc[:, :128] + acc[:, 128:]) * (1.0 / BUCKETS)
        tab_ref[0, g] = tab
        ext = halves(tab)
        for c in range(0, width, CHUNK):
            _, rows, low = factors(sq[pl.ds(base, 8), c : c + CHUNK])
            hi, lo = split(jnp.concatenate(monomials(rows, low), axis=0))
            p = dot(ext, hi)
            num_ref[0, :, c : c + CHUNK] += p[:ROWS] + p[ROWS:] + dot(ext[:ROWS], lo)


def bwd_kernel(
    hashes, groups, inner, q_ref, k_ref, v_ref, valid_ref, proj_ref, num_ref, da_ref, tab_ref, taps_ref,
    dq_ref, dk_ref, dv_ref, dt_ref, sq, sk, gq, gk, cols, xq, xk, dv,
):
    head = pl.program_id(0)
    width = q_ref.shape[2]
    block = width // (groups * inner)
    sq[...] = signs_of(q_ref[0], proj_ref[...])
    sk[...] = signs_of(k_ref[0], proj_ref[...])
    da = da_ref[0]
    v = v_ref[0]
    inv = 1.0 / (num_ref[0, 64:65, :] + HASH_COUNT)
    dn = da * inv
    dd = -jnp.sum(dn * num_ref[0, :64, :], axis=0, keepdims=True) * inv
    cols[...] = columns(dn, dd)
    xq[...] = stacked(dn, dd)
    xk[...] = stacked(v, valid_ref[...])
    dv[...] = jnp.zeros(dv.shape, F32)

    @pl.loop(0, hashes)
    def _(g):
        base = pl.multiple_of(g * 8, 8)
        tabs = beside(tab_ref[0, g])
        acc = None
        for c in range(0, width, CHUNK):
            s8 = sq[pl.ds(base, 8), c : c + CHUNK]
            r, rows, low = factors(s8)
            phi = monomials(rows, low)
            hi, lo = split(jnp.concatenate(phi, axis=0))
            value = cols[c : c + CHUNK, :]
            p = dot(hi, value) + dot(lo, value)
            acc = p if acc is None else acc + p
            d = dot(tabs, xq[:, c : c + CHUNK])
            gq[pl.ds(base, 8), c : c + CHUNK] = sign_grad(r, rows, low, phi, d) * (2.0 - 2.0 * s8 * s8)
        tab = (acc[:, :128] + acc[:, 128:]) * (1.0 / BUCKETS)
        ext = halves(tab)
        tabs = beside(tab)
        for c in range(0, width, CHUNK):
            s8 = sk[pl.ds(base, 8), c : c + CHUNK]
            r, rows, low = factors(s8)
            phi = monomials(rows, low)
            hi, lo = split(jnp.concatenate(phi, axis=0))
            p = dot(ext, hi)
            dv[:, c : c + CHUNK] += p[:ROWS] + p[ROWS:] + dot(ext[:ROWS], lo)
            d = dot(tabs, xk[:, c : c + CHUNK])
            gk[pl.ds(base, 8), c : c + CHUNK] = sign_grad(r, rows, low, phi, d) * (2.0 - 2.0 * s8 * s8)

    back = proj_ref[...].T
    for u_ref, g_ref, o_ref in ((q_ref, gq, dq_ref), (k_ref, gk, dk_ref)):
        u = u_ref[0]
        scale = norm_scale(u)
        g = dot3(back, g_ref[...])
        inside = g - u * (scale * scale * jnp.mean(g * u, axis=0, keepdims=True))
        o_ref[0] = (scale * 0.125) * inside
    natural = reorder(v, inner, groups, block)
    grad = reorder(da, inner, groups, block)
    conv = jnp.zeros(natural.shape, F32)
    for j in range(CONV):
        conv = conv + shifted(grad, HALF - j) * taps_ref[head, j]
        moved = grad * shifted(natural, j - HALF)
        dt_ref[0, j : j + 1, :] = jnp.sum(moved, axis=0, keepdims=True)
    dv_ref[0] = (dv[:64, :] + reorder(conv, groups, inner, block)) * valid_ref[...]


def one(*shape, at=0):
    return pl.BlockSpec((1,) + shape, lambda h: (h + at,) + (0,) * len(shape))


def same(*shape):
    return pl.BlockSpec(shape, lambda h: (0,) * len(shape))


SMEM = pl.BlockSpec(memory_space=pltpu.SMEM)


def attend(qkv, valid, proj, taps, groups, inner):
    heads, width = qkv.shape[0] // 3, qkv.shape[2]
    hashes = proj.shape[0] // 8
    return pl.pallas_call(
        functools.partial(fwd_kernel, hashes, groups, inner),
        grid=(heads,),
        in_specs=[
            one(64, width), one(64, width, at=heads), one(64, width, at=2 * heads),
            same(1, width), same(*proj.shape), SMEM,
        ],
        out_specs=[one(ROWS, width), one(hashes, BUCKETS, 128), one(64, width)],
        out_shape=[
            jax.ShapeDtypeStruct((heads, ROWS, width), F32),
            jax.ShapeDtypeStruct((heads, hashes, BUCKETS, 128), F32),
            jax.ShapeDtypeStruct((heads, 64, width), F32),
        ],
        scratch_shapes=[pltpu.VMEM((hashes * 8, width), F32)] * 2 + [pltpu.VMEM((width, 256), BF)],
        compiler_params=pltpu.CompilerParams(vmem_limit_bytes=VMEM_BYTES),
        name="attend",
    )(qkv, qkv, qkv, valid, proj, taps)


def attend_back(qkv, valid, proj, num, d_attn, tab, taps, groups, inner):
    heads, width = qkv.shape[0] // 3, qkv.shape[2]
    hashes = proj.shape[0] // 8
    return pl.pallas_call(
        functools.partial(bwd_kernel, hashes, groups, inner),
        grid=(heads,),
        in_specs=[
            one(64, width), one(64, width, at=heads), one(64, width, at=2 * heads),
            same(1, width), same(*proj.shape), one(ROWS, width), one(64, width),
            one(hashes, BUCKETS, 128), SMEM,
        ],
        out_specs=[one(64, width)] * 3 + [one(16, width)],
        out_shape=[jax.ShapeDtypeStruct((heads, 64, width), F32)] * 3
        + [jax.ShapeDtypeStruct((heads, 16, width), F32)],
        scratch_shapes=[pltpu.VMEM((hashes * 8, width), F32)] * 4
        + [pltpu.VMEM((width, 256), BF)]
        + [pltpu.VMEM((256, width), BF)] * 2
        + [pltpu.VMEM((ROWS, width), F32)],
        compiler_params=pltpu.CompilerParams(vmem_limit_bytes=VMEM_BYTES),
        name="attend_back",
    )(qkv, qkv, qkv, valid, proj, num, d_attn, tab, taps)


class Line:
    def __init__(self, groups, inner):
        self.groups, self.inner = groups, inner
        index = lax.axis_index("seq")
        self.z, self.c = index // inner, index % inner

    def send(self, x, target):
        pairs = []
        for z in range(self.groups):
            for c in range(self.inner):
                to = target(z, c)
                if to is not None:
                    pairs.append((z * self.inner + c, to[0] * self.inner + to[1]))
        return lax.ppermute(x, "seq", pairs)

    def ordered(self, parts, place):
        count = len(parts)
        whole = jnp.stack(parts)
        return jnp.stack(
            [
                lax.dynamic_index_in_dim(whole, (place - s) % count, 0, keepdims=False)
                for s in range(count)
            ]
        )

    def gather_z(self, x):
        groups = self.groups
        right, left = [x], [x]
        for step in range(1, groups):
            right.append(
                self.send(right[-1], lambda z, c: (z + 1, c) if step - 1 <= z < groups - 1 else None)
            )
            left.append(
                self.send(left[-1], lambda z, c: (z - 1, c) if 0 < z <= groups - step else None)
            )
        parts = [x] + [right[s] + left[groups - s] for s in range(1, groups)]
        return self.ordered(parts, self.z)

    def gather_c(self, x):
        parts = [x] + [
            self.send(x, lambda z, c: (z, (c + s) % self.inner)) for s in range(1, self.inner)
        ]
        return self.ordered(parts, self.c)

    def sum_c(self, x):
        step = 1
        while step < self.inner:
            x = x + self.send(x, lambda z, c: (z, c ^ step))
            step *= 2
        return x

    def share_c(self, x):
        total = lax.dynamic_index_in_dim(x, self.c, 0, keepdims=False)
        for s in range(1, self.inner):
            block = lax.dynamic_index_in_dim(x, (self.c + s) % self.inner, 0, keepdims=False)
            total = total + self.send(block, lambda z, c: (z, (c + s) % self.inner))
        return total

    def swap_z(self, x):
        parts = [lax.dynamic_index_in_dim(x, self.z, 0, keepdims=False)]
        for s in range(1, self.groups):
            block = lax.dynamic_index_in_dim(x, (self.z + s) % self.groups, 0, keepdims=False)
            parts.append(self.send(block, lambda z, c: ((z + s) % self.groups, c)))
        return self.ordered(parts, self.z)


def normalize(x):
    centered = x - jnp.mean(x, axis=-1, keepdims=True)
    scale = lax.rsqrt(jnp.mean(centered * centered, axis=-1, keepdims=True) + 1e-05)
    return centered * scale, scale


def normalize_back(grad, normed, scale):
    mean = jnp.mean(grad, axis=-1, keepdims=True)
    along = jnp.mean(grad * normed, axis=-1, keepdims=True)
    return scale * (grad - mean - normed * along)


def dense(x, attn_t, out_grad, w_out, b_out, gain_one, bias_one, w_up, b_up, w_down, b_down, gain_two, bias_two):
    n1, scale1 = normalize(x + by_weight(attn_t, w_out, 0, 0) + b_out)
    first = n1 * gain_one + bias_one
    hidden = by_weight(first, w_up, 1, 0) + b_up
    cdf = 0.5 + 0.5 * lax.erf(hidden * math.sqrt(0.5))
    inner = hidden * cdf
    n2, scale2 = normalize(first + by_weight(inner, w_down, 1, 0) + b_down)
    output = n2 * gain_two + bias_two
    d_second = normalize_back(out_grad * gain_two, n2, scale2)
    slope = cdf + hidden * (jnp.exp(-0.5 * hidden * hidden) * (1.0 / math.sqrt(2.0 * math.pi)))
    d_hidden = by_weight(d_second, w_down, 1, 1) * slope
    d_first = d_second + by_weight(d_hidden, w_up, 1, 1)
    d_pre = normalize_back(d_first * gain_one, n1, scale1)
    d_hi, d_lo = parts_of(d_pre)
    d_attn_t = contract(w_out, d_hi, 1, 1) + contract(w_out, d_lo, 1, 1)
    grads = dict(
        w_out=outer_sum(attn_t.T, d_pre),
        b_out=jnp.sum(d_pre, axis=0),
        gain_one=jnp.sum(d_first * n1, axis=0),
        bias_one=jnp.sum(d_first, axis=0),
        w_up=outer_sum(first, d_hidden),
        b_up=jnp.sum(d_hidden, axis=0),
        w_down=outer_sum(inner, d_second),
        b_down=jnp.sum(d_second, axis=0),
        gain_two=jnp.sum(out_grad * n2, axis=0),
        bias_two=jnp.sum(out_grad, axis=0),
    )
    return output, d_attn_t, d_pre, grads


def hadamard():
    index = lax.iota(jnp.int32, BUCKETS)
    both = lax.population_count(index[:, None] & index[None, :])
    return jnp.where((both & 1) == 0, 1.0, -1.0).astype(BF)


def per_device(
    inputs, lengths, pad_mask, hash_proj, w_query, b_query, w_key, b_key, w_value, b_value, conv_taps,
    w_out, b_out, gain_one, bias_one, w_up, b_up, w_down, b_down, gain_two, bias_two, out_grad,
):
    count = lax.axis_size("seq")
    groups = math.gcd(HEAD_COUNT, count)
    inner = count // groups
    line = Line(groups, inner)
    heads = HEAD_COUNT // groups
    feats = heads * HEAD_SIZE
    own_hashes = HASH_COUNT // count
    hashes = own_hashes * groups
    tokens = inputs.shape[1]
    width = count * tokens
    x = inputs[0]

    x_line = line.gather_z(x)
    x_all = line.gather_c(x_line).reshape(width, MODEL_WIDTH)
    mask_all = line.gather_c(line.gather_z(pad_mask)).reshape(inner, groups, tokens)
    position = (
        (lax.iota(jnp.int32, groups)[None, :, None] * inner + lax.iota(jnp.int32, inner)[:, None, None])
        * tokens
        + lax.iota(jnp.int32, tokens)[None, None, :]
    )
    valid = ((position < lengths[0]) & (mask_all == 1)).astype(F32).reshape(1, width)

    def head_columns(w):
        return lax.dynamic_slice_in_dim(w, line.z * feats, feats, axis=w.ndim - 1)

    w_qkv = jnp.concatenate([head_columns(w) for w in (w_query, w_key, w_value)], axis=1)
    b_qkv = jnp.concatenate([head_columns(b) for b in (b_query, b_key, b_value)])
    x_hi, x_lo = parts_of(x_all)
    qkv = contract(w_qkv, x_hi, 0, 1) + contract(w_qkv, x_lo, 0, 1) + b_qkv[:, None]
    keep = jnp.concatenate(
        [jnp.ones((2 * feats, 1), F32), jnp.zeros((feats, 1), F32)], axis=0
    )
    qkv = qkv * jnp.where(keep > 0, 1.0, valid)
    qkv = qkv.reshape(3 * heads, HEAD_SIZE, width)
    proj = lax.dynamic_index_in_dim(
        hash_proj.reshape(HEAD_SIZE, groups, inner, own_hashes * HASH_BITS), line.c, 2, keepdims=False
    )
    proj = proj.reshape(HEAD_SIZE, hashes * HASH_BITS).T
    taps = lax.dynamic_slice_in_dim(conv_taps, line.z * heads, heads, axis=0)

    num_part, tab, conv = attend(qkv, valid, proj, taps, groups, inner)
    num = line.sum_c(num_part)
    mixed = num[:, :HEAD_SIZE] / (num[:, HEAD_SIZE : HEAD_SIZE + 1] + HASH_COUNT)
    attn = (mixed + conv).reshape(feats, inner, groups, tokens)
    mine = lax.dynamic_index_in_dim(attn, line.c, 1, keepdims=False)
    attn_t = line.swap_z(mine.transpose(1, 0, 2)).reshape(MODEL_WIDTH, tokens)

    subsets = tab[:, :, :, HEAD_SIZE].reshape(heads * hashes, BUCKETS)
    sub_hi, sub_rest = parts_of(subsets)
    sub_mid, sub_lo = parts_of(subsets - sub_hi.astype(F32))
    signs = hadamard()
    own_counts = contract(sub_hi, signs, 1, 0) + contract(sub_mid, signs, 1, 0) + contract(sub_lo, signs, 1, 0)
    own_counts = own_counts.reshape(heads, groups, own_hashes, BUCKETS).transpose(1, 0, 2, 3)
    counts = line.swap_z(own_counts).reshape(HEAD_COUNT, own_hashes, BUCKETS)

    output, d_attn_t, d_pre, grads = dense(
        x, attn_t, out_grad[0], w_out, b_out, gain_one, bias_one, w_up, b_up, w_down, b_down, gain_two, bias_two
    )
    d_line = line.swap_z(d_attn_t.reshape(groups, feats, tokens))
    d_all = line.gather_c(d_line).transpose(2, 0, 1, 3).reshape(heads, HEAD_SIZE, width)

    first_c = jnp.where(line.c == 0, 1.0, 0.0)
    d_q, d_k, d_v, d_t = attend_back(qkv, valid, proj, num, d_all, tab, taps * first_c, groups, inner)
    d_qkv = jnp.stack([d_q, d_k, d_v]).reshape(3 * feats, inner, groups * tokens)
    d_mine = line.share_c(d_qkv.transpose(1, 0, 2))
    d_taps = jnp.sum(d_t[:, :CONV], axis=2) * first_c

    back = line.swap_z(d_mine.reshape(3 * feats, groups, tokens).transpose(1, 0, 2))
    back = back.reshape(groups, 3, feats, tokens)
    d_x = d_pre
    for i, w in enumerate((w_query, w_key, w_value)):
        d_x = d_x + by_weight(back[:, i].reshape(MODEL_WIDTH, tokens), w, 0, 1)

    dh, dl = parts_of(d_mine)
    xh, xl = parts_of(x_line.reshape(groups * tokens, MODEL_WIDTH))
    d_w = contract(xh, dh, 0, 1) + contract(xl, dh, 0, 1) + contract(xh, dl, 0, 1)
    d_b = jnp.sum(d_mine, axis=1)
    d_cols = jnp.concatenate([d_w, d_b[None, :]], axis=0)
    placed = jnp.zeros((groups, MODEL_WIDTH + 1, 3 * feats), F32)
    placed = lax.dynamic_update_index_in_dim(placed, d_cols, line.z, 0)
    taps_placed = lax.dynamic_update_index_in_dim(
        jnp.zeros((groups, heads, CONV), F32), d_taps, line.z, 0
    )
    both = ("item", "seq")
    summed = lax.psum(placed, both)
    d_conv_taps = lax.psum(taps_placed, both).reshape(HEAD_COUNT, CONV)
    summed = summed.reshape(groups, MODEL_WIDTH + 1, 3, feats).transpose(2, 1, 0, 3)
    summed = summed.reshape(3, MODEL_WIDTH + 1, MODEL_WIDTH)
    names = (
        "w_out", "b_out", "gain_one", "bias_one", "w_up", "b_up", "w_down", "b_down", "gain_two", "bias_two",
    )
    grads = lax.psum(grads, both)
    result = []
    for i in range(3):
        result += [summed[i, :MODEL_WIDTH], summed[i, MODEL_WIDTH]]
    result += [d_conv_taps] + [grads[name] for name in names]
    return (output[None], d_x[None], counts[None], *result)


def solution(mesh):
    tokens = P("item", "seq", None)
    in_specs = (tokens, P("item"), P("item", "seq")) + (P(),) * 18 + (tokens,)
    out_specs = (tokens, tokens, P("item", None, "seq", None)) + (P(),) * 17
    return jax.shard_map(
        per_device, mesh=mesh, in_specs=in_specs, out_specs=out_specs, check_vma=False
    )
```

```python
import functools
import itertools
import math

import jax
import jax.numpy as jnp
from jax import lax
from jax.experimental import pallas as pl
from jax.experimental.pallas import tpu as pltpu
from jax.sharding import Mesh
from jax.sharding import PartitionSpec as P

MODEL_WIDTH = 768
HEAD_COUNT = 12
HEAD_SIZE = 64
HASH_COUNT = 32
HASH_BITS = 8
BUCKETS = 256
EXTRA = 32
CONV = 9
HALF = CONV // 2
ROWS = 80
CHUNK = 256
VMEM_BYTES = 32 * 1024 * 1024
BACK_VMEM = 24 * 1024 * 1024
OUTER_VMEM = 16 * 1024 * 1024
BACK_PARTS = 2

BF = jnp.bfloat16
F32 = jnp.float32


def split(x):
    hi = x.astype(BF)
    return hi, (x - hi.astype(F32)).astype(BF)


def parts_of(x):
    hi = lax.reduce_precision(x, 8, 7)
    return hi.astype(BF), (x - hi).astype(BF)


def dot(a, b):
    return jnp.dot(a, b, preferred_element_type=F32)


def dot3(a, b):
    ah, al = split(a)
    bh, bl = split(b)
    return dot(ah, bh) + dot(ah, bl) + dot(al, bh)


def contract(a, b, i, j):
    return lax.dot_general(a, b, (((i,), (j,)), ((), ())), preferred_element_type=F32)


def by_weight(x, w, i, j):
    hi, lo = parts_of(x)
    return contract(hi, w, i, j) + contract(lo, w, i, j)


def outer_sum(a, b):
    ah, al = parts_of(a)
    bh, bl = parts_of(b)
    return contract(
        jnp.concatenate([ah, al, ah], axis=0), jnp.concatenate([bh, bh, bl], axis=0), 0, 0
    )


def factors(s8):
    w = s8.shape[1]
    r = lax.broadcasted_iota(jnp.int32, (8, w), 0)
    rows = [jnp.broadcast_to(s8[j : j + 1], (8, w)) for j in range(8)]
    low = [jnp.where((r & m) != 0, rows[j], 1.0) for j, m in ((5, 4), (6, 2), (7, 1))]
    return r, rows, low


def monomials(rows, low):
    out = [low[0] * low[1] * low[2]]
    for j in (4, 3, 2, 1, 0):
        out = out + [rows[j] * x for x in out]
    return out


def row_sums(r, parts):
    step = 1
    while len(parts) > 1:
        bit = (r & step) != 0
        parts = [
            jnp.where(bit, b, a) + pltpu.roll(jnp.where(bit, a, b), step, 0)
            for a, b in zip(parts[0::2], parts[1::2])
        ]
        step *= 2
    return parts[0]


def sign_grad(r, rows, low, phi, d):
    c = [d[8 * v : 8 * v + 8] for v in range(32)]
    parts = []
    for j in range(5):
        half = len(c) // 2
        acc = phi[0] * c[half]
        for n in range(1, half):
            acc = acc + phi[n] * c[half + n]
        parts.append(acc)
        c = [c[n] + rows[j] * c[half + n] for n in range(half)]
    m = c[0]
    zero = jnp.zeros_like(m)
    parts.append(jnp.where((r & 4) != 0, m * low[1] * low[2], zero))
    parts.append(jnp.where((r & 2) != 0, m * low[0] * low[2], zero))
    parts.append(jnp.where((r & 1) != 0, m * low[0] * low[1], zero))
    return row_sums(r, parts)


def norm_scale(u):
    return lax.rsqrt(jnp.mean(u * u, axis=0, keepdims=True) + 1e-06)


def signs_of(u, proj):
    return jnp.tanh(2.0 * dot3(proj, u * (norm_scale(u) * 0.125)))


def columns(rows64, row):
    t = jnp.concatenate([rows64, row, jnp.zeros((63, row.shape[1]), F32)], axis=0).T
    return jnp.concatenate(split(t), axis=1)


def stacked(rows64, row):
    width = row.shape[1]
    hi, lo = split(jnp.concatenate([rows64, row, jnp.zeros((15, width), F32)], axis=0))
    return jnp.concatenate([hi, hi, lo, jnp.zeros((16, width), BF)], axis=0)


def beside(tab):
    hi = tab.astype(BF).astype(F32)
    lo = pltpu.roll(tab - hi, ROWS, 1)
    again = pltpu.roll(hi, 2 * ROWS - 128, 1)
    lane = lax.broadcasted_iota(jnp.int32, tab.shape, 1)
    return jnp.concatenate(
        [jnp.where(lane < ROWS, hi, lo), jnp.where(lane < 2 * ROWS - 128, lo, again)], axis=1
    ).astype(BF)


def halves(tab):
    return jnp.concatenate(split(tab.T[:ROWS]), axis=0)


def shifted(x, offset):
    if offset == 0:
        return x
    width = x.shape[1]
    t = lax.broadcasted_iota(jnp.int32, x.shape, 1) + offset
    return jnp.where((t >= 0) & (t < width), pltpu.roll(x, (-offset) % width, 1), 0.0)


def reorder(x, outer, inner, block):
    return jnp.concatenate(
        [
            x[:, (o * inner + i) * block : (o * inner + i + 1) * block]
            for i in range(inner)
            for o in range(outer)
        ],
        axis=1,
    )


def fill_kernel(k_ref, v_ref, valid_ref, proj_ref, *refs):
    tab_ref, sk, cols = refs[-3:]
    hashes, width = tab_ref.shape[1], k_ref.shape[2]
    part = pl.program_id(1)

    @pl.when(part == 0)
    def _():
        sk[...] = signs_of(k_ref[0], proj_ref[...])
        cols[...] = columns(v_ref[0], valid_ref[...])

    for g in range(hashes):
        base = pl.multiple_of((part * hashes + g) * 8, 8)
        acc = None
        for c in range(0, width, CHUNK):
            _, rows, low = factors(sk[pl.ds(base, 8), c : c + CHUNK])
            hi, lo = split(jnp.concatenate(monomials(rows, low), axis=0))
            value = cols[c : c + CHUNK, :]
            p = dot(hi, value) + dot(lo, value)
            acc = p if acc is None else acc + p
        tab = acc[:, :128] + acc[:, 128:]
        if len(refs) > 3:
            tab = tab + refs[0][0, g]
        tab_ref[0, g] = tab


def read_kernel(
    hashes, groups, inner, q_ref, v_ref, tab_ref, proj_ref, taps_ref, num_ref, conv_ref, cnt_ref, sq,
):
    head = pl.program_id(0)
    width = q_ref.shape[2]
    block = width // (groups * inner)
    sq[...] = signs_of(q_ref[0], proj_ref[...])
    num_ref[0] = jnp.zeros(num_ref.shape[1:], F32)
    natural = reorder(v_ref[0], inner, groups, block)
    conv = jnp.zeros(natural.shape, F32)
    for j in range(CONV):
        conv = conv + shifted(natural, j - HALF) * taps_ref[head, j]
    conv_ref[0] = reorder(conv, groups, inner, block)

    @pl.loop(0, hashes)
    def _(g):
        base = pl.multiple_of(g * 8, 8)
        flat = (tab_ref[0, g] * (1.0 / BUCKETS)).T[:ROWS]
        cnt_ref[0, pl.ds(g, 1), :] = flat[64:65]
        ext = jnp.concatenate(split(flat), axis=0)
        for c in range(0, width, CHUNK):
            _, rows, low = factors(sq[pl.ds(base, 8), c : c + CHUNK])
            hi, lo = split(jnp.concatenate(monomials(rows, low), axis=0))
            p = dot(ext, hi)
            num_ref[0, :, c : c + CHUNK] += p[:ROWS] + p[ROWS:] + dot(ext[:ROWS], lo)


def bwd_kernel(
    hashes, groups, inner, with_conv, q_ref, k_ref, v_ref, valid_ref, proj_ref, num_ref, da_ref, tab_ref, taps_ref,
    dq_ref, dk_ref, dv_ref, dt_ref, sq, sk, gq, gk, cols, xq, xk, dv,
):
    width = q_ref.shape[2]
    block = width // (groups * inner)
    sq[...] = signs_of(q_ref[0], proj_ref[...])
    sk[...] = signs_of(k_ref[0], proj_ref[...])
    da = da_ref[0]
    v = v_ref[0]
    inv = 1.0 / (num_ref[0, 64:65, :] + HASH_COUNT)
    dn = da * inv
    dd = -jnp.sum(dn * num_ref[0, :64, :], axis=0, keepdims=True) * inv
    cols[...] = columns(dn, dd)
    xq[...] = stacked(dn, dd)
    xk[...] = stacked(v, valid_ref[...])
    dv[...] = jnp.zeros(dv.shape, F32)

    @pl.loop(0, hashes)
    def _(g):
        base = pl.multiple_of(g * 8, 8)
        tabs = beside(tab_ref[0, g] * (1.0 / BUCKETS))
        acc = None
        for c in range(0, width, CHUNK):
            s8 = sq[pl.ds(base, 8), c : c + CHUNK]
            r, rows, low = factors(s8)
            phi = monomials(rows, low)
            hi, lo = split(jnp.concatenate(phi, axis=0))
            value = cols[c : c + CHUNK, :]
            p = dot(hi, value) + dot(lo, value)
            acc = p if acc is None else acc + p
            d = dot(tabs, xq[:, c : c + CHUNK])
            gq[pl.ds(base, 8), c : c + CHUNK] = sign_grad(r, rows, low, phi, d) * (2.0 - 2.0 * s8 * s8)
        tab = (acc[:, :128] + acc[:, 128:]) * (1.0 / BUCKETS)
        ext = halves(tab)
        tabs = beside(tab)
        for c in range(0, width, CHUNK):
            s8 = sk[pl.ds(base, 8), c : c + CHUNK]
            r, rows, low = factors(s8)
            phi = monomials(rows, low)
            hi, lo = split(jnp.concatenate(phi, axis=0))
            p = dot(ext, hi)
            dv[:, c : c + CHUNK] += p[:ROWS] + p[ROWS:] + dot(ext[:ROWS], lo)
            d = dot(tabs, xk[:, c : c + CHUNK])
            gk[pl.ds(base, 8), c : c + CHUNK] = sign_grad(r, rows, low, phi, d) * (2.0 - 2.0 * s8 * s8)

    back = proj_ref[...].T
    for u_ref, g_ref, o_ref in ((q_ref, gq, dq_ref), (k_ref, gk, dk_ref)):
        u = u_ref[0]
        scale = norm_scale(u)
        g = dot3(back, g_ref[...])
        inside = g - u * (scale * scale * jnp.mean(g * u, axis=0, keepdims=True))
        o_ref[0] = (scale * 0.125) * inside
    total = dv[:64, :]
    if with_conv:
        natural = reorder(v, inner, groups, block)
        grad = reorder(da, inner, groups, block)
        conv = jnp.zeros(natural.shape, F32)
        for j in range(CONV):
            conv = conv + shifted(grad, HALF - j) * taps_ref[0, j]
            moved = grad * shifted(natural, j - HALF)
            dt_ref[j : j + 1, :] = jnp.sum(moved, axis=0, keepdims=True)
        total = total + reorder(conv, groups, inner, block)
    dv_ref[0] = total * valid_ref[...]


def one(*shape, at=0):
    return pl.BlockSpec((1,) + shape, lambda h: (h + at,) + (0,) * len(shape))


def same(*shape):
    return pl.BlockSpec(shape, lambda h: (0,) * len(shape))


SMEM = pl.BlockSpec(memory_space=pltpu.SMEM)


def fill(qkv, valid, proj, tab):
    heads, width = qkv.shape[0] // 3, qkv.shape[2]
    hashes = proj.shape[0] // 8
    parts = 4
    ins = [qkv, qkv, valid, proj] + [tab] * (tab is not None)

    def rows(at):
        return pl.BlockSpec((1, 64, width), lambda h, p: (h + at, 0, 0))

    table = pl.BlockSpec((1, hashes // parts, BUCKETS, 128), lambda h, p: (h, p, 0, 0))
    specs = [
        rows(heads), rows(2 * heads), pl.BlockSpec((1, width), lambda h, p: (0, 0)),
        pl.BlockSpec(proj.shape, lambda h, p: (0, 0)), table,
    ]
    return pl.pallas_call(
        fill_kernel,
        grid=(heads, parts),
        in_specs=specs[: len(ins)],
        out_specs=table,
        out_shape=jax.ShapeDtypeStruct((heads, hashes, BUCKETS, 128), F32),
        scratch_shapes=[pltpu.VMEM((hashes * 8, width), F32), pltpu.VMEM((width, 256), BF)],
        compiler_params=pltpu.CompilerParams(vmem_limit_bytes=OUTER_VMEM),
        cost_estimate=pl.CostEstimate(flops=0, bytes_accessed=0, transcendentals=0),
        name="fill",
    )(*ins)


def read(qkv, tab, proj, taps, groups, inner):
    heads, width = qkv.shape[0] // 3, qkv.shape[2]
    hashes = proj.shape[0] // 8
    return pl.pallas_call(
        functools.partial(read_kernel, hashes, groups, inner),
        grid=(heads,),
        in_specs=[
            one(64, width), one(64, width, at=2 * heads), one(hashes, BUCKETS, 128), same(*proj.shape), SMEM,
        ],
        out_specs=[one(ROWS, width), one(64, width), one(hashes, BUCKETS)],
        out_shape=[
            jax.ShapeDtypeStruct((heads, ROWS, width), F32),
            jax.ShapeDtypeStruct((heads, 64, width), F32),
            jax.ShapeDtypeStruct((heads, hashes, BUCKETS), F32),
        ],
        scratch_shapes=[pltpu.VMEM((hashes * 8, width), F32)],
        compiler_params=pltpu.CompilerParams(vmem_limit_bytes=VMEM_BYTES),
        cost_estimate=pl.CostEstimate(flops=0, bytes_accessed=0, transcendentals=0),
        name="read",
    )(qkv, qkv, tab, proj, taps)


def attend_back(head, part, parts, qkv, valid, proj, num, d_attn, tab, taps, groups, inner):
    heads, width = qkv.shape[0] // 3, qkv.shape[2]
    hashes = proj.shape[0] // 8 // parts

    def pick(*shape, at):
        return pl.BlockSpec((1,) + shape, lambda _: (at,) + (0,) * len(shape))

    return pl.pallas_call(
        functools.partial(bwd_kernel, hashes, groups, inner, part == 0),
        grid=(1,),
        in_specs=[
            pick(64, width, at=head), pick(64, width, at=heads + head), pick(64, width, at=2 * heads + head),
            same(1, width), pl.BlockSpec((hashes * 8, 64), lambda _: (part, 0)),
            pick(ROWS, width, at=head), pick(64, width, at=head),
            pl.BlockSpec((1, hashes, BUCKETS, 128), lambda _: (head, part, 0, 0)), SMEM,
        ],
        out_specs=[pick(64, width, at=0)] * 3 + [same(16, width)],
        out_shape=[jax.ShapeDtypeStruct((1, 64, width), F32)] * 3
        + [jax.ShapeDtypeStruct((16, width), F32)],
        scratch_shapes=[pltpu.VMEM((hashes * 8, width), F32)] * 4
        + [pltpu.VMEM((width, 256), BF)]
        + [pltpu.VMEM((256, width), BF)] * 2
        + [pltpu.VMEM((ROWS, width), F32)],
        compiler_params=pltpu.CompilerParams(vmem_limit_bytes=BACK_VMEM),
        cost_estimate=pl.CostEstimate(flops=0, bytes_accessed=0, transcendentals=0),
        name="attend_back",
    )(qkv, qkv, qkv, valid, proj, num, d_attn, tab, taps)


def copy_kernel(x_ref, o_ref):
    o_ref[...] = x_ref[...]


def widened(x, columns):
    size = MODEL_WIDTH
    return pl.pallas_call(
        copy_kernel,
        grid=(columns // size, 2),
        in_specs=[pl.BlockSpec((size // 2, size), lambda j, i: (j * 2 + i, 0))],
        out_specs=pl.BlockSpec((size // 2, size), lambda j, i: (i, j)),
        out_shape=jax.ShapeDtypeStruct((size, columns), x.dtype),
        compiler_params=pltpu.CompilerParams(vmem_limit_bytes=OUTER_VMEM),
        cost_estimate=pl.CostEstimate(flops=0, bytes_accessed=0, transcendentals=0),
        name="widened",
    )(x)


def rejoin_kernel(c_ref, *refs):
    count = len(refs) - 3
    rows = refs[-1].shape[0]
    for s in range(count):

        @pl.when(pl.program_id(0) == s)
        def _():
            for i in range(3):
                refs[count + i][...] = refs[s][i, :rows]


def rejoined(parts, rows, c):
    count, columns = len(parts), parts[0].shape[2]
    out = pl.BlockSpec((rows, columns), lambda s, c_ref: (lax.rem(c_ref[0] + count - s, count), 0))
    return pl.pallas_call(
        rejoin_kernel,
        grid_spec=pltpu.PrefetchScalarGridSpec(
            num_scalar_prefetch=1,
            grid=(count,),
            in_specs=[pl.BlockSpec(t.shape, lambda *_: (0, 0, 0)) for t in parts],
            out_specs=[out] * 3,
        ),
        out_shape=[jax.ShapeDtypeStruct((count * rows, columns), F32)] * 3,
        compiler_params=pltpu.CompilerParams(vmem_limit_bytes=VMEM_BYTES),
        cost_estimate=pl.CostEstimate(flops=0, bytes_accessed=0, transcendentals=0),
        name="rejoined",
    )(c.reshape(1), *parts)


def copied(x):
    rows, columns = x.shape
    block = rows // 8
    spec = pl.BlockSpec((block, columns), lambda i: (i, 0))
    return pl.pallas_call(
        copy_kernel,
        grid=(8,),
        in_specs=[spec],
        out_specs=spec,
        out_shape=jax.ShapeDtypeStruct(x.shape, x.dtype),
        compiler_params=pltpu.CompilerParams(vmem_limit_bytes=OUTER_VMEM),
        cost_estimate=pl.CostEstimate(flops=0, bytes_accessed=0, transcendentals=0),
        name="copied",
    )(x)


def outer_kernel(inner, c_ref, a_ref, b_ref, *refs):
    *out_refs, whole = refs
    items, rows = out_refs[0].shape[:2]
    ah, al = split(a_ref[...])
    bh, bl = split(b_ref[...])
    dims = (((0,), (0,)), ((), ()))
    whole[...] = (
        lax.dot_general(ah, bh, dims, preferred_element_type=F32)
        + lax.dot_general(al, bh, dims, preferred_element_type=F32)
        + lax.dot_general(ah, bl, dims, preferred_element_type=F32)
    )
    for s, out_ref in enumerate(out_refs):
        start = lax.rem(c_ref[0] + s, inner) * rows
        for i in range(items):
            out_ref[i] = whole[pl.ds(pl.multiple_of(i * inner * rows + start, 8), rows), :]


def outer_blocks(a, b, items, inner, c):
    tokens, wide = a.shape
    block, columns = wide // items, b.shape[1]
    each = 1 if block % 128 == 0 else items
    width = min(columns, MODEL_WIDTH)
    return pl.pallas_call(
        functools.partial(outer_kernel, inner),
        grid=(items // each, columns // width),
        in_specs=[
            SMEM,
            pl.BlockSpec((tokens, each * block), lambda i, j: (0, i)),
            pl.BlockSpec((tokens, width), lambda i, j: (0, j)),
        ],
        out_specs=[pl.BlockSpec((each, block // inner, width), lambda i, j: (i, 0, j))] * inner,
        out_shape=[jax.ShapeDtypeStruct((items, block // inner, columns), F32)] * inner,
        scratch_shapes=[pltpu.VMEM((each * block, width), F32)],
        compiler_params=pltpu.CompilerParams(vmem_limit_bytes=OUTER_VMEM),
        cost_estimate=pl.CostEstimate(flops=0, bytes_accessed=0, transcendentals=0),
        name="outer_blocks",
    )(c.reshape(1), a, b)


def rows_kernel(
    inner, c_ref, first_ref, hidden_ref, attn_ref, pre_ref, second_ref, d_first_ref, n1_ref, n2_ref, grad_ref, *out_refs
):
    s, item, k = (pl.program_id(i) for i in range(3))
    block = (item * inner + lax.rem(c_ref[0] + s, inner)) * pl.num_programs(2) + k
    size = out_refs[0].shape[0]
    each = MODEL_WIDTH // size
    ups = hidden_ref.shape[1] // MODEL_WIDTH * each

    def product(a, b, dims):
        ah, al = split(a)
        bh, bl = split(b)
        return sum(
            lax.dot_general(x, y, (dims, ((), ())), preferred_element_type=F32)
            for x, y in ((ah, bh), (al, bh), (ah, bl))
        )

    def put(value):
        for i, out_ref in enumerate(out_refs):

            @pl.when(s == i)
            def _():
                out_ref[...] = value

    @pl.when(block < ups)
    def _():
        at = pl.multiple_of(lax.rem(block, each) * size, size)
        to = pl.multiple_of(lax.div(block, each) * MODEL_WIDTH, MODEL_WIDTH)
        put(product(first_ref[:, pl.ds(at, size)], hidden_ref[:, pl.ds(to, MODEL_WIDTH)], ((0,), (0,))))

    @pl.when((block >= ups) & (block < ups + each))
    def _():
        at = pl.multiple_of((block - ups) * size, size)
        put(product(attn_ref[pl.ds(at, size), :], pre_ref[...], ((1,), (0,))))

    @pl.when(block == ups + each)
    def _():
        def down(t):
            return jnp.sum(t, axis=0, keepdims=True)

        rows = [
            down(pre_ref[...]), down(d_first_ref[...] * n1_ref[...]), down(d_first_ref[...]), down(second_ref[...]),
            down(grad_ref[...] * n2_ref[...]), down(grad_ref[...]),
        ]
        wide = hidden_ref.shape[1]
        rows += [down(hidden_ref[:, j : j + MODEL_WIDTH]) for j in range(0, wide, MODEL_WIDTH)]
        rows.append(jnp.zeros((size - len(rows), MODEL_WIDTH), F32))
        put(jnp.concatenate(rows))

    @pl.when(block > ups + each)
    def _():
        put(jnp.zeros((size, MODEL_WIDTH), F32))


def outer_rows(first, d_hidden, attn_t, d_pre, others, items, inner, c):
    rows = (d_hidden.shape[1] + MODEL_WIDTH + 256) // (items * inner)
    size = 256 if rows % 256 == 0 else 128
    blocks = rows // size

    def place(i):
        last = items * blocks - 1

        def index(s, item, k, _):
            at = item * blocks + k
            return jnp.where(s == i, at, jnp.where(s > i, last, 0)), 0

        return pl.BlockSpec((size, MODEL_WIDTH), index)

    ins = [first, d_hidden, attn_t, d_pre, *others]
    shape = jax.ShapeDtypeStruct((items * rows, MODEL_WIDTH), F32)
    parts = pl.pallas_call(
        functools.partial(rows_kernel, inner),
        grid_spec=pltpu.PrefetchScalarGridSpec(
            num_scalar_prefetch=1,
            grid=(inner, items, blocks),
            in_specs=[pl.BlockSpec(t.shape, lambda *_: (0, 0)) for t in ins],
            out_specs=[place(i) for i in range(inner)],
        ),
        out_shape=[shape] * inner,
        compiler_params=pltpu.CompilerParams(vmem_limit_bytes=VMEM_BYTES),
        cost_estimate=pl.CostEstimate(flops=0, bytes_accessed=0, transcendentals=0),
        name="outer_rows",
    )(c.reshape(1), *ins)
    return [t.reshape(items, -1, MODEL_WIDTH) for t in parts]


AXES = ("item", "z", "core")
ITEM, Z, C = range(3)


class Grid:
    def __init__(self, sizes):
        self.sizes = sizes
        self.place = tuple(lax.axis_index(name) for name in AXES)
        self.found = []

    def send(self, x, axis, target):
        sizes = self.sizes
        pairs = []
        for source in itertools.product(*(range(n) for n in sizes)):
            to = target(source[axis])
            if to is None:
                continue
            there = source[:axis] + (to,) + source[axis + 1 :]
            flat = [functools.reduce(lambda t, ni: t * ni[0] + ni[1], zip(sizes, p), 0) for p in (source, there)]
            pairs.append(tuple(flat))
        return lax.ppermute(x, AXES, pairs)

    def ordered(self, parts, axis):
        count, own = len(parts), self.place[axis]
        if count == 1:
            return parts
        if count == 2:
            swap = own == 1
            return [jnp.where(swap, parts[1], parts[0]), jnp.where(swap, parts[0], parts[1])]
        whole = jnp.stack(parts)
        return [lax.dynamic_index_in_dim(whole, (own - s) % count, 0, keepdims=False) for s in range(count)]

    def offer(self, x, axis):
        count = self.sizes[axis]
        return [x] + [self.send(x, axis, lambda i: (i + s) % count) for s in range(1, count)]

    def collect(self, parts, axis, dim=None):
        parts = self.ordered(parts, axis)
        return parts if dim is None else jnp.concatenate(parts, axis=dim)

    def spread(self, x, axis):
        return jnp.stack(self.collect(self.offer(x, axis), axis))

    def deal(self, x, axis, dim=0):
        count, own = self.sizes[axis], self.place[axis]
        size = x.shape[dim] // count
        parts = [x]
        for s in range(1, count):
            block = lax.dynamic_slice_in_dim(x, (own + s) % count * size, size, dim)
            parts.append(self.send(block, axis, lambda i: (i + s) % count))
        return parts

    def own_block(self, x, axis, dim):
        size = x.shape[dim] // self.sizes[axis]
        return lax.dynamic_slice_in_dim(x, self.place[axis] * size, size, dim)

    def add(self, parts, axis, dim=0):
        total = self.own_block(parts[0], axis, dim)
        for part in parts[1:]:
            total = total + part
        return total

    def take(self, parts, axis, dim=0):
        return self.ordered([self.own_block(parts[0], axis, dim)] + parts[1:], axis)

    def arrivals(self, axis):
        count = self.sizes[axis]
        return [
            sorted((s, d) for s in range(1, count) for d in (-1, 1) if 0 <= i + d * s < count) for i in range(count)
        ]

    def step_on(self, up, down, axis, step):
        count = self.sizes[axis]
        up = self.send(up, axis, lambda i: i + 1 if step - 1 <= i < count - 1 else None)
        down = self.send(down, axis, lambda i: i - 1 if 0 < i <= count - step else None)
        return up, down

    def arrived(self, came, axis, k):
        own, result = self.place[axis], None
        for i, moves in enumerate(self.arrivals(axis)):
            step, way = moves[k - 1]
            candidate = came[step][(way + 1) // 2]
            result = candidate if result is None else jnp.where(own == i, candidate, result)
        return result

    def places(self, axis):
        count, own = self.sizes[axis], self.place[axis]
        j = lax.iota(jnp.int32, count)
        s = jnp.abs(j - own)
        before = jnp.minimum(s - 1, own) + jnp.minimum(s - 1, count - 1 - own)
        both = ((j > own) & (own >= s)).astype(jnp.int32)
        places = jnp.where(j == own, 0, before + both + 1)
        return [places[i] for i in range(count)]

    def by_index(self, parts, places):
        whole = jnp.stack(parts)
        return [lax.dynamic_index_in_dim(whole, place, 0, keepdims=False) for place in places]


    def dealing(self, x, axis, dim=0):
        count, own = self.sizes[axis], self.place[axis]
        size = x.shape[dim] // count
        blocks = [lax.dynamic_slice_in_dim(x, (own + s) % count * size, size, dim) for s in range(count)]
        return (yield from self.moving(axis, blocks))

    def moving(self, axis, blocks):
        yield axis, blocks
        return (yield)

    def applying(self, function, x):
        yield function, [x]
        return (yield)

    def move(self, axis, blocks_of):
        count = self.sizes[axis]
        result = [[blocks[0]] for blocks in blocks_of]
        for s in range(1, count):
            out = [blocks[s] if len(blocks) > 1 else blocks[0] for blocks in blocks_of]
            if len(out) == 1:
                result[0].append(self.send(out[0], axis, lambda i: (i + s) % count))
                continue
            lane = functools.reduce(math.gcd, (t.shape[1] for t in out))
            lanes = [[t[:, k : k + lane] for k in range(0, t.shape[1], lane)] for t in out]
            whole = self.send(jnp.concatenate(sum(lanes, [])), axis, lambda i: (i + s) % count)
            row = 0
            for t, into in zip(out, result):
                rows, wide = t.shape[0], t.shape[1] // lane
                pieces = [whole[row + k * rows : row + (k + 1) * rows] for k in range(wide)]
                into.append(jnp.concatenate(pieces, axis=1))
                row += rows * wide
        return result

    def reduce(self, blocks):
        blocks = yield blocks
        x = sum((yield from self.moving(C, blocks)))
        scatter = functools.partial(lax.psum_scatter, axis_name="item", scatter_dimension=0, tiled=True)
        x = (yield from self.applying(scatter, x))[0][0]
        x = sum((yield from self.dealing(x, Z)))
        x = self.collect((yield from self.moving(Z, [x])), Z, 0)
        gather = functools.partial(lax.all_gather, axis_name=("item", "core"), axis=0, tiled=True)
        return (yield from self.applying(gather, x))

    def head(self, d_parts, x_parts):
        d_parts = yield d_parts
        d_part = jnp.concatenate([sum(parts) for parts in zip(*d_parts)])
        full = sum(self.collect((yield from self.moving(C, [d_part])), C))
        dh, dl = parts_of(full)
        xh, xl = x_parts
        d_w = contract(xh, dh, 0, 1) + contract(xl, dh, 0, 1) + contract(xh, dl, 0, 1)
        d_b = jnp.sum(full, axis=1)
        self.found.append((d_w, d_b, self.own_block(full, C, 1)))

    def home(self, mine):
        mine = yield mine
        return (yield from self.dealing(mine, Z, 1))

    def tail(self, d_w):
        d_w = yield d_w
        feats = d_w.shape[1] // 3
        x = sum((yield from self.dealing(d_w, ITEM)))
        x = self.collect((yield from self.moving(Z, [x])), Z)
        x = [jnp.concatenate([t[:, i * feats : (i + 1) * feats] for t in x], axis=1) for i in range(3)]
        x = yield from self.moving(ITEM, [jnp.stack(x)])
        return (yield from self.moving(C, [self.collect(x, ITEM, 1)]))


class Steps:
    def __init__(self, grid):
        self.grid, self.live, self.state, self.done = grid, {}, {}, {}

    def add(self, name, sequence):
        self.live[name], self.state[name] = sequence, next(sequence)

    def advance(self, states):
        ready = {}
        for name, state in states.items():
            try:
                ready[name] = self.live[name].send(state)
            except StopIteration as end:
                self.done[name] = end.value
                del self.live[name], self.state[name]
        return {name: how for name, (how, _) in ready.items()}, {name: blocks for name, (_, blocks) in ready.items()}

    def carry(self, hows, blocks):
        came = {}
        for axis in (C, Z, ITEM):
            names = [name for name, how in hows.items() if how == axis]
            alike = [name for name in names if axis == Z and blocks[name][0].shape[1] % 128 == 0 and name != "up"]
            groups = [alike] * bool(alike) + [[name] for name in names if name not in alike]
            for group in groups:
                came.update(zip(group, self.grid.move(axis, [blocks[name] for name in group])))
        for name, how in hows.items():
            if callable(how):
                came[name] = how(blocks[name][0])
                came[name] = [came[name]] if how.func is lax.psum_scatter else came[name]
            next(self.live[name])
            self.state[name] = came[name]

    def start(self, name):
        self.carry(*self.advance({name: self.state[name]}))

    def stage(self, names, held=(), beside=()):
        names = [name for name in names if name in self.live]
        states, held = lax.optimization_barrier(({name: self.state[name] for name in names}, held))
        hows, blocks = self.advance(states)
        blocks, beside = lax.optimization_barrier((blocks, beside))
        self.carry(hows, blocks)
        return held, beside


def normalize(x):
    centered = x - jnp.mean(x, axis=-1, keepdims=True)
    scale = lax.rsqrt(jnp.mean(centered * centered, axis=-1, keepdims=True) + 1e-05)
    return centered * scale, scale


def normalize_back(grad, normed, scale):
    mean = jnp.mean(grad, axis=-1, keepdims=True)
    along = jnp.mean(grad * normed, axis=-1, keepdims=True)
    return scale * (grad - mean - normed * along)


def dense(x, attn_t, out_grad, w_out, b_out, gain_one, bias_one, w_up, b_up, w_down, b_down, gain_two, bias_two):
    n1, scale1 = normalize(x + by_weight(attn_t, w_out, 0, 0) + b_out)
    first = n1 * gain_one + bias_one
    hidden = by_weight(first, w_up, 1, 0) + b_up
    cdf = 0.5 + 0.5 * lax.erf(hidden * math.sqrt(0.5))
    inner = hidden * cdf
    n2, scale2 = normalize(first + by_weight(inner, w_down, 1, 0) + b_down)
    output = n2 * gain_two + bias_two
    d_second = normalize_back(out_grad * gain_two, n2, scale2)
    slope = cdf + hidden * (jnp.exp(-0.5 * hidden * hidden) * (1.0 / math.sqrt(2.0 * math.pi)))
    d_hidden = by_weight(d_second, w_down, 1, 1) * slope
    d_first = d_second + by_weight(d_hidden, w_up, 1, 1)
    d_pre = normalize_back(d_first * gain_one, n1, scale1)
    d_hi, d_lo = parts_of(d_pre)
    d_attn_t = contract(w_out, d_hi, 1, 1) + contract(w_out, d_lo, 1, 1)
    return output, d_attn_t, (d_second, first, d_hidden, attn_t, d_pre, d_first, n1, n2, out_grad, inner)


def hadamard():
    index = lax.iota(jnp.int32, BUCKETS)
    both = lax.population_count(index[:, None] & index[None, :])
    return jnp.where((both & 1) == 0, 1.0, -1.0).astype(BF)


def per_device(
    sizes, inputs, lengths, pad_mask, hash_proj, w_query, b_query, w_key, b_key, w_value, b_value, conv_taps,
    w_out, b_out, gain_one, bias_one, w_up, b_up, w_down, b_down, gain_two, bias_two, out_grad,
):
    grid = Grid(sizes)
    items, groups, inner = sizes
    count = groups * inner
    _, z, c = grid.place
    heads = HEAD_COUNT // groups
    feats = heads * HEAD_SIZE
    own_hashes = HASH_COUNT // count
    hashes = own_hashes * groups
    tokens = inputs.shape[1]
    width = count * tokens
    x = inputs[0]

    position = (z * inner + c) * tokens + lax.iota(jnp.int32, tokens)
    valid = ((position < lengths[0]) & (pad_mask[0] == 1)).astype(F32)
    mask_rows = jnp.pad(valid.reshape(1, tokens), ((0, 7), (0, MODEL_WIDTH - tokens)))

    def head_columns(w):
        return lax.dynamic_slice_in_dim(w, z * feats, feats, axis=w.ndim - 1)

    w_qkv = jnp.concatenate([head_columns(w) for w in (w_query, w_key, w_value)], axis=1)
    b_qkv = jnp.concatenate([head_columns(b) for b in (b_query, b_key, b_value)])

    is_value = lax.iota(jnp.int32, 3 * feats)[:, None] >= 2 * feats

    def project(rows):
        hi, lo = parts_of(rows[:tokens])
        here = rows[tokens : tokens + 1, :tokens]
        products = contract(w_qkv, hi, 0, 1) + contract(w_qkv, lo, 0, 1) + b_qkv[:, None]
        products = jnp.where(is_value, products * here, products)
        products = jnp.concatenate([products, jnp.broadcast_to(here, (8, tokens))])
        return grid.collect(grid.offer(products, C), C, 1)

    proj = lax.dynamic_index_in_dim(
        hash_proj.reshape(HEAD_SIZE, groups, inner, own_hashes * HASH_BITS), c, 2, keepdims=False
    )
    proj = proj.reshape(HEAD_SIZE, hashes * HASH_BITS).T
    taps = lax.dynamic_slice_in_dim(conv_taps, z * heads, heads, axis=0)
    up = down = jnp.concatenate([x, mask_rows])
    came, lines, chunks, tab = [(up, down)], [up], [], None
    places = grid.places(Z)
    for k in range(groups):
        if k:
            up, down, tab, chunks, places = lax.optimization_barrier((up, down, tab, chunks, places))
            came.append((up, down))
            lines.append(grid.arrived(came, Z, k))
        if k < groups - 1:
            up, down = grid.step_on(up, down, Z, k + 1)
        chunk = project(lines[-1])
        chunks.append(chunk)
        per_head = chunk[: 3 * feats].reshape(3 * heads, HEAD_SIZE, -1)
        tab = fill(per_head, chunk[3 * feats : 3 * feats + 1], proj, tab)
    chunks = grid.by_index(chunks, places)
    chunks = jnp.concatenate(
        [t[:, i * tokens : (i + 1) * tokens] for i in range(inner) for t in chunks], axis=1
    )
    qkv, valid = chunks[: 3 * feats].reshape(3 * heads, HEAD_SIZE, width), chunks[3 * feats : 3 * feats + 1]

    num_part, conv, subsets = read(qkv, tab, proj, taps, groups, inner)
    num, step = num_part, 1
    while step < inner:
        num = num + grid.send(num, C, lambda i: i ^ step)
        step *= 2
    lines, num = lax.optimization_barrier((lines, num))
    x_line = jnp.stack(grid.by_index(lines, places))
    half = groups * tokens
    own_num, own_conv = (lax.dynamic_slice_in_dim(t, c * half, half, 2) for t in (num, conv))
    attn = own_num[:, :HEAD_SIZE] / (own_num[:, HEAD_SIZE : HEAD_SIZE + 1] + HASH_COUNT) + own_conv
    attn = grid.deal(attn.reshape(feats, half), Z, dim=1)

    rows = MODEL_WIDTH // inner
    x_line = x_line[:, :tokens].reshape(half, MODEL_WIDTH)
    x_half = parts_of(jnp.concatenate(grid.take(grid.deal(x_line, C, dim=1), C, dim=1)))
    attn, x_half = lax.optimization_barrier((attn, x_half))
    attn_t = jnp.concatenate(grid.take(attn, Z, dim=1))

    subsets = subsets.reshape(heads * hashes, BUCKETS)
    sub_hi, sub_rest = parts_of(subsets)
    sub_mid, sub_lo = parts_of(subsets - sub_hi.astype(F32))
    signs = hadamard()
    own_counts = contract(sub_hi, signs, 1, 0) + contract(sub_mid, signs, 1, 0) + contract(sub_lo, signs, 1, 0)
    own_counts = own_counts.reshape(heads, groups, own_hashes, BUCKETS).transpose(1, 0, 2, 3)

    steps = Steps(grid)
    output, d_attn_t, held = dense(
        x, attn_t, out_grad[0],
        w_out, b_out, gain_one, bias_one, w_up, b_up, w_down, b_down, gain_two, bias_two,
    )
    d_line = jnp.concatenate([d_attn_t.reshape(groups, feats, tokens), own_counts.reshape(groups, -1, tokens)], axis=1)
    d_line = [lax.dynamic_index_in_dim(d_line, (z + s) % groups, 0, keepdims=False) for s in range(groups)]
    d_line, held = lax.optimization_barrier((d_line, held))
    d_line = [d_line[0]] + [grid.send(t, Z, lambda i: (i + s) % groups) for s, t in enumerate(d_line[1:], 1)]
    d_second, first, d_hidden, attn_t, d_pre, d_first, n1, n2, cotangent, inside = held
    steps.add("down", grid.reduce(outer_blocks(inside, d_second, items, inner, c)))
    steps.start("down")
    others = (d_second, d_first, n1, n2, cotangent)
    rest = outer_rows(first, d_hidden, attn_t, d_pre, others, items, inner, c)
    d_line, rest, steps.state["down"] = lax.optimization_barrier((d_line, rest, steps.state["down"]))
    steps.add("rest", grid.reduce(rest))
    steps.start("rest")

    def enter(d_line):
        d_line = grid.ordered(d_line, Z)
        own = jnp.concatenate([t[:feats] for t in d_line], axis=1)
        counts = jnp.stack([t[feats:] for t in d_line]).reshape(HEAD_COUNT, own_hashes, BUCKETS)
        return grid.collect(grid.offer(own, C), C, 1).reshape(heads, HEAD_SIZE, width), counts

    d_all, counts = enter(d_line)

    plan = [["down"], ["rest"], ["down", "head0"], ["down"], ["down", "rest", "head0", "head1"], ["rest"]]
    first_c = jnp.where(c == 0, 1.0, 0.0)
    found, last = [], ()
    for call in range(heads * BACK_PARTS):
        head, part = call // BACK_PARTS, call % BACK_PARTS
        if call < len(plan):
            last, d_all = steps.stage(plan[call], last, d_all)
            if call:
                found.append(last)
        own_taps = taps[head : head + 1] * first_c
        last = attend_back(head, part, BACK_PARTS, qkv, valid, proj, num, d_all, tab, own_taps, groups, inner)
        if part == BACK_PARTS - 1:
            whole_head = [f[:3] for f in found[head * BACK_PARTS :]] + [last[:3]]
            steps.add(f"head{head}", grid.head([[t[0] for t in f] for f in whole_head], x_half))
    found.append(last)
    d_t = [jnp.sum(found[head * BACK_PARTS][3][:CONV], axis=1) * first_c for head in range(heads)]
    last_head = f"head{heads - 1}"
    steps.stage(["head1", last_head])
    steps.stage([last_head])
    d_w = [t[0].reshape(-1, 3, HEAD_SIZE) for t in grid.found]
    d_w = jnp.stack(d_w, axis=2).reshape(-1, 3 * feats)
    d_b = jnp.stack([t[1].reshape(3, HEAD_SIZE) for t in grid.found], axis=1).reshape(-1)
    d_t = jnp.pad(jnp.concatenate(d_t), (0, 3 * feats - heads * CONV))
    rows = MODEL_WIDTH // inner
    below = jnp.pad(jnp.stack([d_b, d_t]), ((0, EXTRA - 2), (0, 0)))
    steps.add("tail", grid.tail(jnp.concatenate([d_w, below])))
    mine = jnp.concatenate([t[2] for t in grid.found])
    steps.add("home", grid.home(mine))
    steps.stage(["tail", "rest"])
    steps.stage(["tail", "home"])
    steps.stage(["tail", "down"])
    d_down = copied(steps.done["down"])
    steps.stage(["tail", "home", "rest"], d_down)
    rest, wide, back = steps.done["rest"], w_up.shape[1], steps.done["home"]
    d_up = widened(rest, wide)
    d_out, last_rows = rest[wide : wide + MODEL_WIDTH], rest[wide + MODEL_WIDTH :]
    back = [t.reshape(heads, 3, HEAD_SIZE, tokens) for t in grid.ordered(back, Z)]
    back = [jnp.concatenate([t[:, i] for t in back]).reshape(MODEL_WIDTH, tokens) for i in range(3)]
    d_x = held[4]
    for i, w in enumerate((w_query, w_key, w_value)):
        d_x = d_x + by_weight(back[i], w, 0, 1)
    (d_x, d_up, d_out), _ = steps.stage(["tail"], (d_x, d_up, d_out))
    tail = steps.done["tail"]
    weights = rejoined(tail, rows, c)
    below = tail[0][:, rows:]
    for s in range(1, inner):
        below = jnp.where(c == s, tail[s][:, rows:], below)
    d_b = below[:, 0]
    d_conv_taps = below[0, 1].reshape(groups, feats)[:, : heads * CONV].reshape(HEAD_COUNT, CONV)
    names = ("b_out", "gain_one", "bias_one", "b_down", "gain_two", "bias_two")
    vectors = dict(zip(names, last_rows))
    vectors["b_up"] = last_rows[len(names) : len(names) + wide // MODEL_WIDTH].reshape(-1)

    result = []
    for i in range(3):
        result += [weights[i], d_b[i]]
    result += [
        d_conv_taps, d_out, vectors["b_out"], vectors["gain_one"], vectors["bias_one"], d_up, vectors["b_up"],
        d_down, vectors["b_down"], vectors["gain_two"], vectors["bias_two"],
    ]
    return (output[None], d_x[None], counts[None], *result)


def solution(mesh):
    items, count = mesh.shape["item"], mesh.shape["seq"]
    groups = math.gcd(HEAD_COUNT, count)
    sizes = (items, groups, count // groups)
    seq = ("z", "core")
    tokens = P("item", seq, None)
    in_specs = (tokens, P("item"), P("item", seq)) + (P(),) * 18 + (tokens,)
    out_specs = (tokens, tokens, P("item", None, seq, None)) + (P(),) * 17
    return jax.shard_map(
        functools.partial(per_device, sizes),
        mesh=Mesh(mesh.devices.reshape(sizes), AXES),
        in_specs=in_specs,
        out_specs=out_specs,
        check_vma=False,
    )
```

```python
import functools
import itertools
import math

import jax
import jax.numpy as jnp
from jax import lax
from jax.experimental import pallas as pl
from jax.experimental.pallas import tpu as pltpu
from jax.sharding import Mesh
from jax.sharding import PartitionSpec as P

MODEL_WIDTH = 768
HEAD_COUNT = 12
HEAD_SIZE = 64
HASH_COUNT = 32
HASH_BITS = 8
BUCKETS = 256
EXTRA = 32
CONV = 9
HALF = CONV // 2
ROWS = 80
CHUNK = 256
VMEM_BYTES = 32 * 1024 * 1024
BACK_VMEM = 60 * 1024 * 1024
OUTER_VMEM = 16 * 1024 * 1024
BACK_PARTS = 2

BF = jnp.bfloat16
F32 = jnp.float32


def split(x):
    hi = x.astype(BF)
    return hi, (x - hi.astype(F32)).astype(BF)


def parts_of(x):
    hi = lax.reduce_precision(x, 8, 7)
    return hi.astype(BF), (x - hi).astype(BF)


def dot(a, b):
    return jnp.dot(a, b, preferred_element_type=F32)


def dot3(a, b):
    ah, al = split(a)
    bh, bl = split(b)
    return dot(ah, bh) + dot(ah, bl) + dot(al, bh)


def contract(a, b, i, j):
    return lax.dot_general(a, b, (((i,), (j,)), ((), ())), preferred_element_type=F32)


def by_weight(x, w, i, j):
    hi, lo = parts_of(x)
    return contract(hi, w, i, j) + contract(lo, w, i, j)


def outer_sum(a, b):
    ah, al = parts_of(a)
    bh, bl = parts_of(b)
    return contract(
        jnp.concatenate([ah, al, ah], axis=0), jnp.concatenate([bh, bh, bl], axis=0), 0, 0
    )


def factors(s8):
    w = s8.shape[1]
    r = lax.broadcasted_iota(jnp.int32, (8, w), 0)
    rows = [jnp.broadcast_to(s8[j : j + 1], (8, w)) for j in range(8)]
    low = [jnp.where((r & m) != 0, rows[j], 1.0) for j, m in ((5, 4), (6, 2), (7, 1))]
    return r, rows, low


def monomials(rows, low):
    out = [low[0] * low[1] * low[2]]
    for j in (4, 3, 2, 1, 0):
        out = out + [rows[j] * x for x in out]
    return out


def row_sums(r, parts):
    step = 1
    while len(parts) > 1:
        bit = (r & step) != 0
        parts = [
            jnp.where(bit, b, a) + pltpu.roll(jnp.where(bit, a, b), step, 0)
            for a, b in zip(parts[0::2], parts[1::2])
        ]
        step *= 2
    return parts[0]


def sign_grad(r, rows, low, phi, d):
    c = [d[8 * v : 8 * v + 8] for v in range(32)]
    parts = []
    for j in range(5):
        half = len(c) // 2
        acc = phi[0] * c[half]
        for n in range(1, half):
            acc = acc + phi[n] * c[half + n]
        parts.append(acc)
        c = [c[n] + rows[j] * c[half + n] for n in range(half)]
    m = c[0]
    zero = jnp.zeros_like(m)
    parts.append(jnp.where((r & 4) != 0, m * low[1] * low[2], zero))
    parts.append(jnp.where((r & 2) != 0, m * low[0] * low[2], zero))
    parts.append(jnp.where((r & 1) != 0, m * low[0] * low[1], zero))
    return row_sums(r, parts)


def norm_scale(u):
    return lax.rsqrt(jnp.mean(u * u, axis=0, keepdims=True) + 1e-06)


def signs_of(u, proj):
    return jnp.tanh(2.0 * dot3(proj, u * (norm_scale(u) * 0.125)))


def columns(rows64, row):
    t = jnp.concatenate([rows64, row, jnp.zeros((63, row.shape[1]), F32)], axis=0).T
    return jnp.concatenate(split(t), axis=1)


def stacked(rows64, row):
    width = row.shape[1]
    hi, lo = split(jnp.concatenate([rows64, row, jnp.zeros((15, width), F32)], axis=0))
    return jnp.concatenate([hi, hi, lo, jnp.zeros((16, width), BF)], axis=0)


def beside(tab):
    hi = tab.astype(BF).astype(F32)
    lo = pltpu.roll(tab - hi, ROWS, 1)
    again = pltpu.roll(hi, 2 * ROWS - 128, 1)
    lane = lax.broadcasted_iota(jnp.int32, tab.shape, 1)
    return jnp.concatenate(
        [jnp.where(lane < ROWS, hi, lo), jnp.where(lane < 2 * ROWS - 128, lo, again)], axis=1
    ).astype(BF)


def halves(tab):
    return jnp.concatenate(split(tab.T[:ROWS]), axis=0)


def shifted(x, offset):
    if offset == 0:
        return x
    width = x.shape[1]
    t = lax.broadcasted_iota(jnp.int32, x.shape, 1) + offset
    return jnp.where((t >= 0) & (t < width), pltpu.roll(x, (-offset) % width, 1), 0.0)


def reorder(x, outer, inner, block):
    return jnp.concatenate(
        [
            x[:, (o * inner + i) * block : (o * inner + i + 1) * block]
            for i in range(inner)
            for o in range(outer)
        ],
        axis=1,
    )


def fill_kernel(k_ref, v_ref, valid_ref, proj_ref, *refs):
    tab_ref, sk, cols = refs[-3:]
    hashes, width = tab_ref.shape[1], k_ref.shape[2]
    part = pl.program_id(1)

    @pl.when(part == 0)
    def _():
        sk[...] = signs_of(k_ref[0], proj_ref[...])
        cols[...] = columns(v_ref[0], valid_ref[...])

    for g in range(hashes):
        base = pl.multiple_of((part * hashes + g) * 8, 8)
        acc = None
        for c in range(0, width, CHUNK):
            _, rows, low = factors(sk[pl.ds(base, 8), c : c + CHUNK])
            hi, lo = split(jnp.concatenate(monomials(rows, low), axis=0))
            value = cols[c : c + CHUNK, :]
            p = dot(hi, value) + dot(lo, value)
            acc = p if acc is None else acc + p
        tab = acc[:, :128] + acc[:, 128:]
        if len(refs) > 3:
            tab = tab + refs[0][0, g]
        tab_ref[0, g] = tab


def read_kernel(
    hashes, groups, inner, q_ref, v_ref, tab_ref, proj_ref, taps_ref, num_ref, conv_ref, cnt_ref, sq,
):
    head = pl.program_id(0)
    width = q_ref.shape[2]
    block = width // (groups * inner)
    sq[...] = signs_of(q_ref[0], proj_ref[...])
    num_ref[0] = jnp.zeros(num_ref.shape[1:], F32)
    natural = reorder(v_ref[0], inner, groups, block)
    conv = jnp.zeros(natural.shape, F32)
    for j in range(CONV):
        conv = conv + shifted(natural, j - HALF) * taps_ref[head, j]
    conv_ref[0] = reorder(conv, groups, inner, block)

    @pl.loop(0, hashes)
    def _(g):
        base = pl.multiple_of(g * 8, 8)
        flat = (tab_ref[0, g] * (1.0 / BUCKETS)).T[:ROWS]
        cnt_ref[0, pl.ds(g, 1), :] = flat[64:65]
        ext = jnp.concatenate(split(flat), axis=0)
        for c in range(0, width, CHUNK):
            _, rows, low = factors(sq[pl.ds(base, 8), c : c + CHUNK])
            hi, lo = split(jnp.concatenate(monomials(rows, low), axis=0))
            p = dot(ext, hi)
            num_ref[0, :, c : c + CHUNK] += p[:ROWS] + p[ROWS:] + dot(ext[:ROWS], lo)


def bwd_kernel(
    hashes, groups, inner, head, part, qkv_hbm, valid_ref, proj_ref, num_hbm, da_hbm, tab_hbm, taps_ref, *refs
):
    before_hbm = refs[0] if part else None
    out_hbm, dt_ref, q_ref, k_ref, v_ref, num_ref, da_ref, tab_ref, before_ref, sq, sk, gq, gk, cols, xq, xk, dv, sems = refs[
        1 if part else 0 :
    ]
    heads, width = num_hbm.shape[0], q_ref.shape[2]
    block = width // (groups * inner)
    sources = (
        qkv_hbm.at[head], qkv_hbm.at[heads + head], qkv_hbm.at[2 * heads + head], num_hbm.at[head], da_hbm.at[head],
        tab_hbm.at[head, part * hashes : (part + 1) * hashes],
    )
    targets = (q_ref, k_ref, v_ref, num_ref, da_ref, tab_ref)
    copies = [
        pltpu.make_async_copy(source, target.at[0], sems.at[i])
        for i, (source, target) in enumerate(zip(sources, targets))
    ]
    if part:
        copies.append(pltpu.make_async_copy(before_hbm, before_ref, sems.at[6]))
    for copy in copies:
        copy.start()
    copies[0].wait()
    sq[...] = signs_of(q_ref[0], proj_ref[...])
    copies[1].wait()
    sk[...] = signs_of(k_ref[0], proj_ref[...])
    for copy in copies[2:]:
        copy.wait()
    da = da_ref[0]
    v = v_ref[0]
    inv = 1.0 / (num_ref[0, 64:65, :] + HASH_COUNT)
    dn = da * inv
    dd = -jnp.sum(dn * num_ref[0, :64, :], axis=0, keepdims=True) * inv
    cols[...] = columns(dn, dd)
    xq[...] = stacked(dn, dd)
    xk[...] = stacked(v, valid_ref[...])
    dv[...] = jnp.zeros(dv.shape, F32)

    @pl.loop(0, hashes)
    def _(g):
        base = pl.multiple_of(g * 8, 8)
        tabs = beside(tab_ref[0, g] * (1.0 / BUCKETS))
        acc = None
        for c in range(0, width, CHUNK):
            s8 = sq[pl.ds(base, 8), c : c + CHUNK]
            r, rows, low = factors(s8)
            phi = monomials(rows, low)
            hi, lo = split(jnp.concatenate(phi, axis=0))
            value = cols[c : c + CHUNK, :]
            p = dot(hi, value) + dot(lo, value)
            acc = p if acc is None else acc + p
            d = dot(tabs, xq[:, c : c + CHUNK])
            gq[pl.ds(base, 8), c : c + CHUNK] = sign_grad(r, rows, low, phi, d) * (2.0 - 2.0 * s8 * s8)
        tab = (acc[:, :128] + acc[:, 128:]) * (1.0 / BUCKETS)
        ext = halves(tab)
        tabs = beside(tab)
        for c in range(0, width, CHUNK):
            s8 = sk[pl.ds(base, 8), c : c + CHUNK]
            r, rows, low = factors(s8)
            phi = monomials(rows, low)
            hi, lo = split(jnp.concatenate(phi, axis=0))
            p = dot(ext, hi)
            dv[:, c : c + CHUNK] += p[:ROWS] + p[ROWS:] + dot(ext[:ROWS], lo)
            d = dot(tabs, xk[:, c : c + CHUNK])
            gk[pl.ds(base, 8), c : c + CHUNK] = sign_grad(r, rows, low, phi, d) * (2.0 - 2.0 * s8 * s8)

    back = proj_ref[...].T
    copies = [
        pltpu.make_async_copy(source.at[0], out_hbm.at[64 * i : 64 * i + 64], sems.at[i])
        for i, source in enumerate((q_ref, k_ref, v_ref))
    ]
    total = dv[:64, :]
    if part == 0:
        natural = reorder(v, inner, groups, block)
        grad = reorder(da, inner, groups, block)
        conv = jnp.zeros(natural.shape, F32)
        for j in range(CONV):
            conv = conv + shifted(grad, HALF - j) * taps_ref[0, j]
            moved = grad * shifted(natural, j - HALF)
            dt_ref[j : j + 1, :] = jnp.sum(moved, axis=0, keepdims=True)
        total = total + reorder(conv, groups, inner, block)
    total = total * valid_ref[...]
    v_ref[0] = total + before_ref[128:, :] if part else total
    copies[2].start()
    for i, (u_ref, g_ref) in enumerate(((q_ref, gq), (k_ref, gk))):
        u = u_ref[0]
        scale = norm_scale(u)
        g = dot3(back, g_ref[...])
        inside = g - u * (scale * scale * jnp.mean(g * u, axis=0, keepdims=True))
        grad = (scale * 0.125) * inside
        u_ref[0] = grad + before_ref[64 * i : 64 * i + 64, :] if part else grad
        copies[i].start()
    for copy in copies:
        copy.wait()


def one(*shape, at=0):
    return pl.BlockSpec((1,) + shape, lambda h: (h + at,) + (0,) * len(shape))


def same(*shape):
    return pl.BlockSpec(shape, lambda h: (0,) * len(shape))


SMEM = pl.BlockSpec(memory_space=pltpu.SMEM)


def fill(qkv, valid, proj, tab):
    heads, width = qkv.shape[0] // 3, qkv.shape[2]
    hashes = proj.shape[0] // 8
    parts = 4
    ins = [qkv, qkv, valid, proj] + [tab] * (tab is not None)

    def rows(at):
        return pl.BlockSpec((1, 64, width), lambda h, p: (h + at, 0, 0))

    table = pl.BlockSpec((1, hashes // parts, BUCKETS, 128), lambda h, p: (h, p, 0, 0))
    specs = [
        rows(heads), rows(2 * heads), pl.BlockSpec((1, width), lambda h, p: (0, 0)),
        pl.BlockSpec(proj.shape, lambda h, p: (0, 0)), table,
    ]
    return pl.pallas_call(
        fill_kernel,
        grid=(heads, parts),
        in_specs=specs[: len(ins)],
        out_specs=table,
        out_shape=jax.ShapeDtypeStruct((heads, hashes, BUCKETS, 128), F32),
        scratch_shapes=[pltpu.VMEM((hashes * 8, width), F32), pltpu.VMEM((width, 256), BF)],
        compiler_params=pltpu.CompilerParams(vmem_limit_bytes=OUTER_VMEM),
        cost_estimate=pl.CostEstimate(flops=0, bytes_accessed=0, transcendentals=0),
        name="fill",
    )(*ins)


def read(qkv, tab, proj, taps, groups, inner):
    heads, width = qkv.shape[0] // 3, qkv.shape[2]
    hashes = proj.shape[0] // 8
    return pl.pallas_call(
        functools.partial(read_kernel, hashes, groups, inner),
        grid=(heads,),
        in_specs=[
            one(64, width), one(64, width, at=2 * heads), one(hashes, BUCKETS, 128), same(*proj.shape), SMEM,
        ],
        out_specs=[one(ROWS, width), one(64, width), one(hashes, BUCKETS)],
        out_shape=[
            jax.ShapeDtypeStruct((heads, ROWS, width), F32),
            jax.ShapeDtypeStruct((heads, 64, width), F32),
            jax.ShapeDtypeStruct((heads, hashes, BUCKETS), F32),
        ],
        scratch_shapes=[pltpu.VMEM((hashes * 8, width), F32)],
        compiler_params=pltpu.CompilerParams(vmem_limit_bytes=VMEM_BYTES),
        cost_estimate=pl.CostEstimate(flops=0, bytes_accessed=0, transcendentals=0),
        name="read",
    )(qkv, qkv, tab, proj, taps)


def attend_back(head, part, parts, qkv, valid, proj, num, d_attn, tab, taps, before, groups, inner):
    width = qkv.shape[2]
    hashes = proj.shape[0] // 8 // parts
    hbm = pl.BlockSpec(memory_space=pltpu.HBM)
    rows = pltpu.VMEM((1, 64, width), F32)
    ins = [qkv, valid, proj, num, d_attn, tab, taps] + [before] * (part > 0)
    specs = [hbm, same(1, width), pl.BlockSpec((hashes * 8, 64), lambda _: (part, 0)), hbm, hbm, hbm, SMEM, hbm]
    return pl.pallas_call(
        functools.partial(bwd_kernel, hashes, groups, inner, head, part),
        grid=(1,),
        in_specs=specs[: len(ins)],
        out_specs=[hbm, same(16, width)],
        out_shape=[jax.ShapeDtypeStruct((192, width), F32), jax.ShapeDtypeStruct((16, width), F32)],
        scratch_shapes=[rows] * 3
        + [pltpu.VMEM((1, ROWS, width), F32), rows, pltpu.VMEM((1, hashes, BUCKETS, 128), F32)]
        + [pltpu.VMEM((192, width), F32)]
        + [pltpu.VMEM((hashes * 8, width), F32)] * 4
        + [pltpu.VMEM((width, 256), BF)]
        + [pltpu.VMEM((256, width), BF)] * 2
        + [pltpu.VMEM((ROWS, width), F32), pltpu.SemaphoreType.DMA((7,))],
        compiler_params=pltpu.CompilerParams(vmem_limit_bytes=BACK_VMEM),
        cost_estimate=pl.CostEstimate(flops=0, bytes_accessed=0, transcendentals=0),
        name="attend_back",
    )(*ins)


def weights_kernel(count, c_ref, *refs):
    parts, (hi_ref, lo_ref, w_ref, sum_ref, mine_ref, full_ref) = refs[:count], refs[count:]
    full = parts[0][...]
    for part in parts[1:]:
        full = full + part[...]
    full_ref[...] = full
    fh, fl = split(full)
    w_ref[...] = dot(fh, hi_ref[...]) + dot(fl, hi_ref[...]) + dot(fh, lo_ref[...])
    sum_ref[...] = jnp.broadcast_to(jnp.sum(full, axis=1, keepdims=True), sum_ref.shape)
    size = mine_ref.shape[1]
    mine_ref[...] = full_ref[:, pl.ds(pl.multiple_of(c_ref[0] * size, 128), size)]


def weights_of(parts, x_parts, c):
    features, tokens = parts[0].shape
    ins = [*parts, *x_parts]
    vmem = pl.BlockSpec(memory_space=pltpu.VMEM)
    return pl.pallas_call(
        functools.partial(weights_kernel, len(parts)),
        in_specs=[SMEM] + [vmem] * len(ins),
        out_specs=[vmem] * 3,
        out_shape=[
            jax.ShapeDtypeStruct((features, x_parts[0].shape[1]), F32),
            jax.ShapeDtypeStruct((features, 128), F32),
            jax.ShapeDtypeStruct((features, tokens // len(parts)), F32),
        ],
        scratch_shapes=[pltpu.VMEM((features, tokens), F32)],
        compiler_params=pltpu.CompilerParams(vmem_limit_bytes=VMEM_BYTES),
        cost_estimate=pl.CostEstimate(flops=0, bytes_accessed=0, transcendentals=0),
        name="weights_of",
    )(c.reshape(1), *ins)


def copy_kernel(x_ref, o_ref):
    o_ref[...] = x_ref[...]


def widened(x, columns):
    size = MODEL_WIDTH
    return pl.pallas_call(
        copy_kernel,
        grid=(columns // size, 2),
        in_specs=[pl.BlockSpec((size // 2, size), lambda j, i: (j * 2 + i, 0))],
        out_specs=pl.BlockSpec((size // 2, size), lambda j, i: (i, j)),
        out_shape=jax.ShapeDtypeStruct((size, columns), x.dtype),
        compiler_params=pltpu.CompilerParams(vmem_limit_bytes=OUTER_VMEM),
        cost_estimate=pl.CostEstimate(flops=0, bytes_accessed=0, transcendentals=0),
        name="widened",
    )(x)


def rejoin_kernel(c_ref, *refs):
    count = len(refs) - 3
    rows = refs[-1].shape[0]
    for s in range(count):

        @pl.when(pl.program_id(0) == s)
        def _():
            for i in range(3):
                refs[count + i][...] = refs[s][i, :rows]


def rejoined(parts, rows, c):
    count, columns = len(parts), parts[0].shape[2]
    out = pl.BlockSpec((rows, columns), lambda s, c_ref: (lax.rem(c_ref[0] + count - s, count), 0))
    return pl.pallas_call(
        rejoin_kernel,
        grid_spec=pltpu.PrefetchScalarGridSpec(
            num_scalar_prefetch=1,
            grid=(count,),
            in_specs=[pl.BlockSpec(t.shape, lambda *_: (0, 0, 0)) for t in parts],
            out_specs=[out] * 3,
        ),
        out_shape=[jax.ShapeDtypeStruct((count * rows, columns), F32)] * 3,
        compiler_params=pltpu.CompilerParams(vmem_limit_bytes=VMEM_BYTES),
        cost_estimate=pl.CostEstimate(flops=0, bytes_accessed=0, transcendentals=0),
        name="rejoined",
    )(c.reshape(1), *parts)


def copied(x):
    rows, columns = x.shape
    block = rows // 8
    spec = pl.BlockSpec((block, columns), lambda i: (i, 0))
    return pl.pallas_call(
        copy_kernel,
        grid=(8,),
        in_specs=[spec],
        out_specs=spec,
        out_shape=jax.ShapeDtypeStruct(x.shape, x.dtype),
        compiler_params=pltpu.CompilerParams(vmem_limit_bytes=OUTER_VMEM),
        cost_estimate=pl.CostEstimate(flops=0, bytes_accessed=0, transcendentals=0),
        name="copied",
    )(x)


def outer_kernel(inner, c_ref, a_ref, b_ref, *refs):
    *out_refs, whole = refs
    items, rows = out_refs[0].shape[:2]
    ah, al = split(a_ref[...])
    bh, bl = split(b_ref[...])
    dims = (((0,), (0,)), ((), ()))
    whole[...] = (
        lax.dot_general(ah, bh, dims, preferred_element_type=F32)
        + lax.dot_general(al, bh, dims, preferred_element_type=F32)
        + lax.dot_general(ah, bl, dims, preferred_element_type=F32)
    )
    for s, out_ref in enumerate(out_refs):
        start = lax.rem(c_ref[0] + s, inner) * rows
        for i in range(items):
            out_ref[i] = whole[pl.ds(pl.multiple_of(i * inner * rows + start, 8), rows), :]


def outer_blocks(a, b, items, inner, c):
    tokens, wide = a.shape
    block, columns = wide // items, b.shape[1]
    each = 1 if block % 128 == 0 else items
    width = min(columns, MODEL_WIDTH)
    return pl.pallas_call(
        functools.partial(outer_kernel, inner),
        grid=(items // each, columns // width),
        in_specs=[
            SMEM,
            pl.BlockSpec((tokens, each * block), lambda i, j: (0, i)),
            pl.BlockSpec((tokens, width), lambda i, j: (0, j)),
        ],
        out_specs=[pl.BlockSpec((each, block // inner, width), lambda i, j: (i, 0, j))] * inner,
        out_shape=[jax.ShapeDtypeStruct((items, block // inner, columns), F32)] * inner,
        scratch_shapes=[pltpu.VMEM((each * block, width), F32)],
        compiler_params=pltpu.CompilerParams(vmem_limit_bytes=OUTER_VMEM),
        cost_estimate=pl.CostEstimate(flops=0, bytes_accessed=0, transcendentals=0),
        name="outer_blocks",
    )(c.reshape(1), a, b)


def rows_kernel(
    inner, c_ref, first_ref, hidden_ref, attn_ref, pre_ref, second_ref, d_first_ref, n1_ref, n2_ref, grad_ref, *out_refs
):
    s, item, k = (pl.program_id(i) for i in range(3))
    block = (item * inner + lax.rem(c_ref[0] + s, inner)) * pl.num_programs(2) + k
    size = out_refs[0].shape[0]
    each = MODEL_WIDTH // size
    ups = hidden_ref.shape[1] // MODEL_WIDTH * each

    def product(a, b, dims):
        ah, al = split(a)
        bh, bl = split(b)
        return sum(
            lax.dot_general(x, y, (dims, ((), ())), preferred_element_type=F32)
            for x, y in ((ah, bh), (al, bh), (ah, bl))
        )

    def put(value):
        for i, out_ref in enumerate(out_refs):

            @pl.when(s == i)
            def _():
                out_ref[...] = value

    @pl.when(block < ups)
    def _():
        at = pl.multiple_of(lax.rem(block, each) * size, size)
        to = pl.multiple_of(lax.div(block, each) * MODEL_WIDTH, MODEL_WIDTH)
        put(product(first_ref[:, pl.ds(at, size)], hidden_ref[:, pl.ds(to, MODEL_WIDTH)], ((0,), (0,))))

    @pl.when((block >= ups) & (block < ups + each))
    def _():
        at = pl.multiple_of((block - ups) * size, size)
        put(product(attn_ref[pl.ds(at, size), :], pre_ref[...], ((1,), (0,))))

    @pl.when(block == ups + each)
    def _():
        def down(t):
            return jnp.sum(t, axis=0, keepdims=True)

        rows = [
            down(pre_ref[...]), down(d_first_ref[...] * n1_ref[...]), down(d_first_ref[...]), down(second_ref[...]),
            down(grad_ref[...] * n2_ref[...]), down(grad_ref[...]),
        ]
        wide = hidden_ref.shape[1]
        rows += [down(hidden_ref[:, j : j + MODEL_WIDTH]) for j in range(0, wide, MODEL_WIDTH)]
        rows.append(jnp.zeros((size - len(rows), MODEL_WIDTH), F32))
        put(jnp.concatenate(rows))

    @pl.when(block > ups + each)
    def _():
        put(jnp.zeros((size, MODEL_WIDTH), F32))


def outer_rows(first, d_hidden, attn_t, d_pre, others, items, inner, c):
    rows = (d_hidden.shape[1] + MODEL_WIDTH + 256) // (items * inner)
    size = 256 if rows % 256 == 0 else 128
    blocks = rows // size

    def place(i):
        last = items * blocks - 1

        def index(s, item, k, _):
            at = item * blocks + k
            return jnp.where(s == i, at, jnp.where(s > i, last, 0)), 0

        return pl.BlockSpec((size, MODEL_WIDTH), index)

    ins = [first, d_hidden, attn_t, d_pre, *others]
    shape = jax.ShapeDtypeStruct((items * rows, MODEL_WIDTH), F32)
    parts = pl.pallas_call(
        functools.partial(rows_kernel, inner),
        grid_spec=pltpu.PrefetchScalarGridSpec(
            num_scalar_prefetch=1,
            grid=(inner, items, blocks),
            in_specs=[pl.BlockSpec(t.shape, lambda *_: (0, 0)) for t in ins],
            out_specs=[place(i) for i in range(inner)],
        ),
        out_shape=[shape] * inner,
        compiler_params=pltpu.CompilerParams(vmem_limit_bytes=VMEM_BYTES),
        cost_estimate=pl.CostEstimate(flops=0, bytes_accessed=0, transcendentals=0),
        name="outer_rows",
    )(c.reshape(1), *ins)
    return [t.reshape(items, -1, MODEL_WIDTH) for t in parts]


AXES = ("item", "z", "core")
ITEM, Z, C = range(3)


class Grid:
    def __init__(self, sizes):
        self.sizes = sizes
        self.place = tuple(lax.axis_index(name) for name in AXES)
        self.found = []

    def send(self, x, axis, target):
        sizes = self.sizes
        pairs = []
        for source in itertools.product(*(range(n) for n in sizes)):
            to = target(source[axis])
            if to is None:
                continue
            there = source[:axis] + (to,) + source[axis + 1 :]
            flat = [functools.reduce(lambda t, ni: t * ni[0] + ni[1], zip(sizes, p), 0) for p in (source, there)]
            pairs.append(tuple(flat))
        return lax.ppermute(x, AXES, pairs)

    def ordered(self, parts, axis):
        count, own = len(parts), self.place[axis]
        if count == 1:
            return parts
        if count == 2:
            swap = own == 1
            return [jnp.where(swap, parts[1], parts[0]), jnp.where(swap, parts[0], parts[1])]
        whole = jnp.stack(parts)
        return [lax.dynamic_index_in_dim(whole, (own - s) % count, 0, keepdims=False) for s in range(count)]

    def offer(self, x, axis):
        count = self.sizes[axis]
        return [x] + [self.send(x, axis, lambda i: (i + s) % count) for s in range(1, count)]

    def collect(self, parts, axis, dim=None):
        parts = self.ordered(parts, axis)
        return parts if dim is None else jnp.concatenate(parts, axis=dim)

    def spread(self, x, axis):
        return jnp.stack(self.collect(self.offer(x, axis), axis))

    def deal(self, x, axis, dim=0):
        count, own = self.sizes[axis], self.place[axis]
        size = x.shape[dim] // count
        parts = [x]
        for s in range(1, count):
            block = lax.dynamic_slice_in_dim(x, (own + s) % count * size, size, dim)
            parts.append(self.send(block, axis, lambda i: (i + s) % count))
        return parts

    def own_block(self, x, axis, dim):
        size = x.shape[dim] // self.sizes[axis]
        return lax.dynamic_slice_in_dim(x, self.place[axis] * size, size, dim)

    def add(self, parts, axis, dim=0):
        total = self.own_block(parts[0], axis, dim)
        for part in parts[1:]:
            total = total + part
        return total

    def take(self, parts, axis, dim=0):
        return self.ordered([self.own_block(parts[0], axis, dim)] + parts[1:], axis)

    def arrivals(self, axis):
        count = self.sizes[axis]
        return [
            sorted((s, d) for s in range(1, count) for d in (-1, 1) if 0 <= i + d * s < count) for i in range(count)
        ]

    def step_on(self, up, down, axis, step):
        count = self.sizes[axis]
        up = self.send(up, axis, lambda i: i + 1 if step - 1 <= i < count - 1 else None)
        down = self.send(down, axis, lambda i: i - 1 if 0 < i <= count - step else None)
        return up, down

    def arrived(self, came, axis, k):
        own, result = self.place[axis], None
        for i, moves in enumerate(self.arrivals(axis)):
            step, way = moves[k - 1]
            candidate = came[step][(way + 1) // 2]
            result = candidate if result is None else jnp.where(own == i, candidate, result)
        return result

    def places(self, axis):
        count, own = self.sizes[axis], self.place[axis]
        j = lax.iota(jnp.int32, count)
        s = jnp.abs(j - own)
        before = jnp.minimum(s - 1, own) + jnp.minimum(s - 1, count - 1 - own)
        both = ((j > own) & (own >= s)).astype(jnp.int32)
        places = jnp.where(j == own, 0, before + both + 1)
        return [places[i] for i in range(count)]

    def by_index(self, parts, places):
        whole = jnp.stack(parts)
        return [lax.dynamic_index_in_dim(whole, place, 0, keepdims=False) for place in places]


    def dealing(self, x, axis, dim=0):
        count, own = self.sizes[axis], self.place[axis]
        size = x.shape[dim] // count
        blocks = [lax.dynamic_slice_in_dim(x, (own + s) % count * size, size, dim) for s in range(count)]
        return (yield from self.moving(axis, blocks))

    def moving(self, axis, blocks):
        yield axis, blocks
        return (yield)

    def applying(self, function, x):
        yield function, [x]
        return (yield)

    def move(self, axis, blocks_of):
        count = self.sizes[axis]
        result = [[blocks[0]] for blocks in blocks_of]
        for s in range(1, count):
            out = [blocks[s] if len(blocks) > 1 else blocks[0] for blocks in blocks_of]
            if len(out) == 1:
                result[0].append(self.send(out[0], axis, lambda i: (i + s) % count))
                continue
            lane = functools.reduce(math.gcd, (t.shape[1] for t in out))
            lanes = [[t[:, k : k + lane] for k in range(0, t.shape[1], lane)] for t in out]
            whole = self.send(jnp.concatenate(sum(lanes, [])), axis, lambda i: (i + s) % count)
            row = 0
            for t, into in zip(out, result):
                rows, wide = t.shape[0], t.shape[1] // lane
                pieces = [whole[row + k * rows : row + (k + 1) * rows] for k in range(wide)]
                into.append(jnp.concatenate(pieces, axis=1))
                row += rows * wide
        return result

    def reduce(self, blocks):
        blocks = yield blocks
        x = sum((yield from self.moving(C, blocks)))
        scatter = functools.partial(lax.psum_scatter, axis_name="item", scatter_dimension=0, tiled=True)
        x = (yield from self.applying(scatter, x))[0][0]
        x = sum((yield from self.dealing(x, Z)))
        x = self.collect((yield from self.moving(Z, [x])), Z, 0)
        gather = functools.partial(lax.all_gather, axis_name=("item", "core"), axis=0, tiled=True)
        return (yield from self.applying(gather, x))

    def head(self, d_part, x_parts):
        d_part = yield d_part
        parts = yield from self.moving(C, [d_part])
        self.found.append(weights_of(parts, x_parts, self.place[C]))

    def home(self, mine):
        mine = yield mine
        return (yield from self.dealing(mine, Z, 1))

    def tail(self, d_w):
        d_w = yield d_w
        feats = d_w.shape[1] // 3
        x = sum((yield from self.dealing(d_w, ITEM)))
        x = self.collect((yield from self.moving(Z, [x])), Z)
        x = [jnp.concatenate([t[:, i * feats : (i + 1) * feats] for t in x], axis=1) for i in range(3)]
        x = yield from self.moving(ITEM, [jnp.stack(x)])
        return (yield from self.moving(C, [self.collect(x, ITEM, 1)]))


class Steps:
    def __init__(self, grid):
        self.grid, self.live, self.state, self.done = grid, {}, {}, {}

    def add(self, name, sequence):
        self.live[name], self.state[name] = sequence, next(sequence)

    def advance(self, states):
        ready = {}
        for name, state in states.items():
            try:
                ready[name] = self.live[name].send(state)
            except StopIteration as end:
                self.done[name] = end.value
                del self.live[name], self.state[name]
        return {name: how for name, (how, _) in ready.items()}, {name: blocks for name, (_, blocks) in ready.items()}

    def carry(self, hows, blocks):
        came = {}
        for axis in (C, Z, ITEM):
            names = [name for name, how in hows.items() if how == axis]
            alike = [name for name in names if axis == Z and blocks[name][0].shape[1] % 128 == 0 and name != "up"]
            groups = [alike] * bool(alike) + [[name] for name in names if name not in alike]
            for group in groups:
                came.update(zip(group, self.grid.move(axis, [blocks[name] for name in group])))
        for name, how in hows.items():
            if callable(how):
                came[name] = how(blocks[name][0])
                came[name] = [came[name]] if how.func is lax.psum_scatter else came[name]
            next(self.live[name])
            self.state[name] = came[name]

    def start(self, name):
        self.carry(*self.advance({name: self.state[name]}))

    def stage(self, names, held=(), beside=()):
        names = [name for name in names if name in self.live]
        states, held = lax.optimization_barrier(({name: self.state[name] for name in names}, held))
        hows, blocks = self.advance(states)
        blocks, beside = lax.optimization_barrier((blocks, beside))
        self.carry(hows, blocks)
        return held, beside


def normalize(x):
    centered = x - jnp.mean(x, axis=-1, keepdims=True)
    scale = lax.rsqrt(jnp.mean(centered * centered, axis=-1, keepdims=True) + 1e-05)
    return centered * scale, scale


def normalize_back(grad, normed, scale):
    mean = jnp.mean(grad, axis=-1, keepdims=True)
    along = jnp.mean(grad * normed, axis=-1, keepdims=True)
    return scale * (grad - mean - normed * along)


def dense(x, attn_t, out_grad, w_out, b_out, gain_one, bias_one, w_up, b_up, w_down, b_down, gain_two, bias_two):
    n1, scale1 = normalize(x + by_weight(attn_t, w_out, 0, 0) + b_out)
    first = n1 * gain_one + bias_one
    hidden = by_weight(first, w_up, 1, 0) + b_up
    cdf = 0.5 + 0.5 * lax.erf(hidden * math.sqrt(0.5))
    inner = hidden * cdf
    n2, scale2 = normalize(first + by_weight(inner, w_down, 1, 0) + b_down)
    output = n2 * gain_two + bias_two
    d_second = normalize_back(out_grad * gain_two, n2, scale2)
    slope = cdf + hidden * (jnp.exp(-0.5 * hidden * hidden) * (1.0 / math.sqrt(2.0 * math.pi)))
    d_hidden = by_weight(d_second, w_down, 1, 1) * slope
    d_first = d_second + by_weight(d_hidden, w_up, 1, 1)
    d_pre = normalize_back(d_first * gain_one, n1, scale1)
    d_hi, d_lo = parts_of(d_pre)
    d_attn_t = contract(w_out, d_hi, 1, 1) + contract(w_out, d_lo, 1, 1)
    return output, d_attn_t, (d_second, first, d_hidden, attn_t, d_pre, d_first, n1, n2, out_grad, inner)


def hadamard():
    index = lax.iota(jnp.int32, BUCKETS)
    both = lax.population_count(index[:, None] & index[None, :])
    return jnp.where((both & 1) == 0, 1.0, -1.0).astype(BF)


def per_device(
    sizes, inputs, lengths, pad_mask, hash_proj, w_query, b_query, w_key, b_key, w_value, b_value, conv_taps,
    w_out, b_out, gain_one, bias_one, w_up, b_up, w_down, b_down, gain_two, bias_two, out_grad,
):
    grid = Grid(sizes)
    items, groups, inner = sizes
    count = groups * inner
    _, z, c = grid.place
    heads = HEAD_COUNT // groups
    feats = heads * HEAD_SIZE
    own_hashes = HASH_COUNT // count
    hashes = own_hashes * groups
    tokens = inputs.shape[1]
    width = count * tokens
    x = inputs[0]

    position = (z * inner + c) * tokens + lax.iota(jnp.int32, tokens)
    valid = ((position < lengths[0]) & (pad_mask[0] == 1)).astype(F32)
    mask_rows = jnp.pad(valid.reshape(1, tokens), ((0, 7), (0, MODEL_WIDTH - tokens)))

    def head_columns(w):
        return lax.dynamic_slice_in_dim(w, z * feats, feats, axis=w.ndim - 1)

    w_qkv = jnp.concatenate([head_columns(w) for w in (w_query, w_key, w_value)], axis=1)
    b_qkv = jnp.concatenate([head_columns(b) for b in (b_query, b_key, b_value)])

    is_value = lax.iota(jnp.int32, 3 * feats)[:, None] >= 2 * feats

    def project(rows):
        hi, lo = parts_of(rows[:tokens])
        here = rows[tokens : tokens + 1, :tokens]
        products = contract(w_qkv, hi, 0, 1) + contract(w_qkv, lo, 0, 1) + b_qkv[:, None]
        products = jnp.where(is_value, products * here, products)
        products = jnp.concatenate([products, jnp.broadcast_to(here, (8, tokens))])
        return grid.collect(grid.offer(products, C), C, 1)

    proj = lax.dynamic_index_in_dim(
        hash_proj.reshape(HEAD_SIZE, groups, inner, own_hashes * HASH_BITS), c, 2, keepdims=False
    )
    proj = proj.reshape(HEAD_SIZE, hashes * HASH_BITS).T
    taps = lax.dynamic_slice_in_dim(conv_taps, z * heads, heads, axis=0)
    up = down = jnp.concatenate([x, mask_rows])
    came, lines, chunks, tab = [(up, down)], [up], [], None
    places = grid.places(Z)
    for k in range(groups):
        if k:
            up, down, tab, chunks, places, taps = lax.optimization_barrier((up, down, tab, chunks, places, taps))
            came.append((up, down))
            lines.append(grid.arrived(came, Z, k))
        if k < groups - 1:
            up, down = grid.step_on(up, down, Z, k + 1)
        chunk = project(lines[-1])
        chunks.append(chunk)
        per_head = chunk[: 3 * feats].reshape(3 * heads, HEAD_SIZE, -1)
        tab = fill(per_head, chunk[3 * feats : 3 * feats + 1], proj, tab)
    tab, chunks = lax.optimization_barrier((tab, chunks))
    chunks = grid.by_index(chunks, places)
    chunks = jnp.concatenate(
        [t[:, i * tokens : (i + 1) * tokens] for i in range(inner) for t in chunks], axis=1
    )
    qkv, valid = chunks[: 3 * feats].reshape(3 * heads, HEAD_SIZE, width), chunks[3 * feats : 3 * feats + 1]

    num_part, conv, subsets = read(qkv, tab, proj, taps, groups, inner)
    num, step = num_part, 1
    while step < inner:
        num = num + grid.send(num, C, lambda i: i ^ step)
        step *= 2
    lines, num = lax.optimization_barrier((lines, num))
    x_line = jnp.stack(grid.by_index(lines, places))
    half = groups * tokens
    own_num, own_conv = (lax.dynamic_slice_in_dim(t, c * half, half, 2) for t in (num, conv))
    attn = own_num[:, :HEAD_SIZE] / (own_num[:, HEAD_SIZE : HEAD_SIZE + 1] + HASH_COUNT) + own_conv
    attn = grid.deal(attn.reshape(feats, half), Z, dim=1)

    rows = MODEL_WIDTH // inner
    x_line = x_line[:, :tokens].reshape(half, MODEL_WIDTH)
    x_half = parts_of(jnp.concatenate(grid.take(grid.deal(x_line, C, dim=1), C, dim=1)))
    attn, x_half = lax.optimization_barrier((attn, x_half))
    attn_t = jnp.concatenate(grid.take(attn, Z, dim=1))

    subsets = subsets.reshape(heads * hashes, BUCKETS)
    sub_hi, sub_rest = parts_of(subsets)
    sub_mid, sub_lo = parts_of(subsets - sub_hi.astype(F32))
    signs = hadamard()
    own_counts = contract(sub_hi, signs, 1, 0) + contract(sub_mid, signs, 1, 0) + contract(sub_lo, signs, 1, 0)
    own_counts = own_counts.reshape(heads, groups, own_hashes, BUCKETS).transpose(1, 0, 2, 3)

    steps = Steps(grid)
    output, d_attn_t, held = dense(
        x, attn_t, out_grad[0],
        w_out, b_out, gain_one, bias_one, w_up, b_up, w_down, b_down, gain_two, bias_two,
    )
    d_line = jnp.concatenate([d_attn_t.reshape(groups, feats, tokens), own_counts.reshape(groups, -1, tokens)], axis=1)
    d_line = [lax.dynamic_index_in_dim(d_line, (z + s) % groups, 0, keepdims=False) for s in range(groups)]
    d_line, held = lax.optimization_barrier((d_line, held))
    d_line = [d_line[0]] + [grid.send(t, Z, lambda i: (i + s) % groups) for s, t in enumerate(d_line[1:], 1)]
    d_second, first, d_hidden, attn_t, d_pre, d_first, n1, n2, cotangent, inside = held
    steps.add("down", grid.reduce(outer_blocks(inside, d_second, items, inner, c)))
    steps.start("down")
    others = (d_second, d_first, n1, n2, cotangent)
    rest = outer_rows(first, d_hidden, attn_t, d_pre, others, items, inner, c)
    d_line, rest, steps.state["down"] = lax.optimization_barrier((d_line, rest, steps.state["down"]))
    steps.add("rest", grid.reduce(rest))
    steps.start("rest")

    def enter(d_line):
        d_line = grid.ordered(d_line, Z)
        own = jnp.concatenate([t[:feats] for t in d_line], axis=1)
        counts = jnp.stack([t[feats:] for t in d_line]).reshape(HEAD_COUNT, own_hashes, BUCKETS)
        return grid.collect(grid.offer(own, C), C, 1).reshape(heads, HEAD_SIZE, width), counts

    d_all, counts = enter(d_line)

    plan = [["down"], ["rest"], ["down", "head0"], ["down"], ["down", "rest", "head0", "head1"], ["rest"]]
    first_c = jnp.where(c == 0, 1.0, 0.0)

    def staged(names, held=(), beside=()):
        before, count = grid.found, len(grid.found)
        (held, ready), beside = steps.stage(names, (held, before), beside)
        grid.found = ready + before[count:]
        return held, beside

    found, last = [], ()
    for call in range(heads * BACK_PARTS):
        head, part = call // BACK_PARTS, call % BACK_PARTS
        if call < len(plan):
            last, d_all = staged(plan[call], last, d_all)
            if call:
                found.append(last)
        own_taps = taps[head : head + 1] * first_c
        before = last[0] if part else None
        last = attend_back(head, part, BACK_PARTS, qkv, valid, proj, num, d_all, tab, own_taps, before, groups, inner)
        if part == BACK_PARTS - 1:
            steps.add(f"head{head}", grid.head(last[0], x_half))
    found.append(last)
    d_t = [jnp.sum(found[head * BACK_PARTS][1][:CONV], axis=1) * first_c for head in range(heads)]
    last_head = f"head{heads - 1}"
    others = [name for name in steps.live if name.startswith("head") and name != last_head]
    staged(others + [last_head, "rest"])
    staged([last_head])
    steps.add("home", grid.home(jnp.concatenate([t[2] for t in grid.found])))
    d_w = jnp.stack([t[0].reshape(3, HEAD_SIZE, -1) for t in grid.found], axis=1).reshape(3 * feats, -1).T
    d_b = jnp.stack([t[1][:, 0].reshape(3, HEAD_SIZE) for t in grid.found], axis=1).reshape(-1)
    d_t = jnp.pad(jnp.concatenate(d_t), (0, 3 * feats - heads * CONV))
    rows = MODEL_WIDTH // inner
    below = jnp.pad(jnp.stack([d_b, d_t]), ((0, EXTRA - 2), (0, 0)))
    steps.add("tail", grid.tail(jnp.concatenate([d_w, below])))
    def input_part(blocks, first_head):
        count = blocks[0].shape[0] // (3 * HEAD_SIZE)
        total = 0.0
        for i, w in enumerate((w_query, w_key, w_value)):
            spans = [slice((k * 3 + i) * HEAD_SIZE, (k * 3 + i + 1) * HEAD_SIZE) for k in range(count)]
            d = jnp.concatenate([t[span] for t in blocks for span in spans])
            w = w.reshape(MODEL_WIDTH, groups, heads, HEAD_SIZE)[:, :, first_head : first_head + count]
            total = total + by_weight(d, w.reshape(MODEL_WIDTH, -1), 0, 1)
        return total

    steps.stage(["tail"])
    steps.stage(["tail"])
    steps.stage(["tail", "down", "home"])
    d_down = copied(steps.done["down"])
    steps.advance({"rest": steps.state["rest"]})
    rest, wide = steps.done["rest"], w_up.shape[1]
    d_up = widened(rest, wide)
    d_out, last_rows = rest[wide : wide + MODEL_WIDTH], rest[wide + MODEL_WIDTH :]
    (d_down, d_up, d_out, last_rows), _ = steps.stage(["tail", "home"], (d_down, d_up, d_out, last_rows))
    d_x = held[4] + input_part(grid.ordered(steps.done["home"], Z), 0)
    d_x, _ = steps.stage(["tail"], d_x)
    tail = steps.done["tail"]
    weights = rejoined(tail, rows, c)
    below = tail[0][:, rows:]
    for s in range(1, inner):
        below = jnp.where(c == s, tail[s][:, rows:], below)
    d_b = below[:, 0]
    d_conv_taps = below[0, 1].reshape(groups, feats)[:, : heads * CONV].reshape(HEAD_COUNT, CONV)
    names = ("b_out", "gain_one", "bias_one", "b_down", "gain_two", "bias_two")
    vectors = dict(zip(names, last_rows))
    vectors["b_up"] = last_rows[len(names) : len(names) + wide // MODEL_WIDTH].reshape(-1)

    result = []
    for i in range(3):
        result += [weights[i], d_b[i]]
    result += [
        d_conv_taps, d_out, vectors["b_out"], vectors["gain_one"], vectors["bias_one"], d_up, vectors["b_up"],
        d_down, vectors["b_down"], vectors["gain_two"], vectors["bias_two"],
    ]
    return (output[None], d_x[None], counts[None], *result)


def solution(mesh):
    items, count = mesh.shape["item"], mesh.shape["seq"]
    groups = math.gcd(HEAD_COUNT, count)
    sizes = (items, groups, count // groups)
    seq = ("z", "core")
    tokens = P("item", seq, None)
    in_specs = (tokens, P("item"), P("item", seq)) + (P(),) * 18 + (tokens,)
    out_specs = (tokens, tokens, P("item", None, seq, None)) + (P(),) * 17
    return jax.shard_map(
        functools.partial(per_device, sizes),
        mesh=Mesh(mesh.devices.reshape(sizes), AXES),
        in_specs=in_specs,
        out_specs=out_specs,
        check_vma=False,
    )
```

```python
import functools
import itertools
import math

import jax
import jax.numpy as jnp
from jax import lax
from jax.experimental import pallas as pl
from jax.experimental.pallas import tpu as pltpu
from jax.sharding import Mesh
from jax.sharding import PartitionSpec as P

MODEL_WIDTH = 768
HEAD_COUNT = 12
HEAD_SIZE = 64
HASH_COUNT = 32
HASH_BITS = 8
BUCKETS = 256
EXTRA = 32
CONV = 9
HALF = CONV // 2
ROWS = 80
CHUNK = 256
VMEM_BYTES = 32 * 1024 * 1024
BACK_VMEM = 60 * 1024 * 1024
OUTER_VMEM = 16 * 1024 * 1024
BACK_PARTS = 2

BF = jnp.bfloat16
F32 = jnp.float32


def split(x):
    hi = x.astype(BF)
    return hi, (x - hi.astype(F32)).astype(BF)


def parts_of(x):
    hi = lax.reduce_precision(x, 8, 7)
    return hi.astype(BF), (x - hi).astype(BF)


def dot(a, b):
    return jnp.dot(a, b, preferred_element_type=F32)


def dot3(a, b):
    ah, al = split(a)
    bh, bl = split(b)
    return dot(ah, bh) + dot(ah, bl) + dot(al, bh)


def contract(a, b, i, j):
    return lax.dot_general(a, b, (((i,), (j,)), ((), ())), preferred_element_type=F32)


def by_weight(x, w, i, j):
    hi, lo = parts_of(x)
    return contract(hi, w, i, j) + contract(lo, w, i, j)


def outer_sum(a, b):
    ah, al = parts_of(a)
    bh, bl = parts_of(b)
    return contract(
        jnp.concatenate([ah, al, ah], axis=0), jnp.concatenate([bh, bh, bl], axis=0), 0, 0
    )


def factors(s8):
    w = s8.shape[1]
    r = lax.broadcasted_iota(jnp.int32, (8, w), 0)
    rows = [jnp.broadcast_to(s8[j : j + 1], (8, w)) for j in range(8)]
    low = [jnp.where((r & m) != 0, rows[j], 1.0) for j, m in ((5, 4), (6, 2), (7, 1))]
    return r, rows, low


def monomials(rows, low):
    out = [low[0] * low[1] * low[2]]
    for j in (4, 3, 2, 1, 0):
        out = out + [rows[j] * x for x in out]
    return out


def row_sums(r, parts):
    step = 1
    while len(parts) > 1:
        bit = (r & step) != 0
        parts = [
            jnp.where(bit, b, a) + pltpu.roll(jnp.where(bit, a, b), step, 0)
            for a, b in zip(parts[0::2], parts[1::2])
        ]
        step *= 2
    return parts[0]


def sign_grad(r, rows, low, phi, d):
    c = [d[8 * v : 8 * v + 8] for v in range(32)]
    parts = []
    for j in range(5):
        half = len(c) // 2
        acc = phi[0] * c[half]
        for n in range(1, half):
            acc = acc + phi[n] * c[half + n]
        parts.append(acc)
        c = [c[n] + rows[j] * c[half + n] for n in range(half)]
    m = c[0]
    zero = jnp.zeros_like(m)
    parts.append(jnp.where((r & 4) != 0, m * low[1] * low[2], zero))
    parts.append(jnp.where((r & 2) != 0, m * low[0] * low[2], zero))
    parts.append(jnp.where((r & 1) != 0, m * low[0] * low[1], zero))
    return row_sums(r, parts)


def norm_scale(u):
    return lax.rsqrt(jnp.mean(u * u, axis=0, keepdims=True) + 1e-06)


def signs_of(u, proj):
    return jnp.tanh(2.0 * dot3(proj, u * (norm_scale(u) * 0.125)))


def columns(rows64, row):
    t = jnp.concatenate([rows64, row, jnp.zeros((63, row.shape[1]), F32)], axis=0).T
    return jnp.concatenate(split(t), axis=1)


def stacked(rows64, row):
    width = row.shape[1]
    hi, lo = split(jnp.concatenate([rows64, row, jnp.zeros((15, width), F32)], axis=0))
    return jnp.concatenate([hi, hi, lo, jnp.zeros((16, width), BF)], axis=0)


def beside(tab):
    hi = tab.astype(BF).astype(F32)
    lo = pltpu.roll(tab - hi, ROWS, 1)
    again = pltpu.roll(hi, 2 * ROWS - 128, 1)
    lane = lax.broadcasted_iota(jnp.int32, tab.shape, 1)
    return jnp.concatenate(
        [jnp.where(lane < ROWS, hi, lo), jnp.where(lane < 2 * ROWS - 128, lo, again)], axis=1
    ).astype(BF)


def halves(tab):
    return jnp.concatenate(split(tab.T[:ROWS]), axis=0)


def shifted(x, offset):
    if offset == 0:
        return x
    width = x.shape[1]
    t = lax.broadcasted_iota(jnp.int32, x.shape, 1) + offset
    return jnp.where((t >= 0) & (t < width), pltpu.roll(x, (-offset) % width, 1), 0.0)


def reorder(x, outer, inner, block):
    return jnp.concatenate(
        [
            x[:, (o * inner + i) * block : (o * inner + i + 1) * block]
            for i in range(inner)
            for o in range(outer)
        ],
        axis=1,
    )


def fill_kernel(k_ref, v_ref, valid_ref, proj_ref, *refs):
    tab_ref, sk, cols = refs[-3:]
    hashes, width = tab_ref.shape[1], k_ref.shape[2]
    part = pl.program_id(1)

    @pl.when(part == 0)
    def _():
        sk[...] = signs_of(k_ref[0], proj_ref[...])
        cols[...] = columns(v_ref[0], valid_ref[...])

    for g in range(hashes):
        base = pl.multiple_of((part * hashes + g) * 8, 8)
        acc = None
        for c in range(0, width, CHUNK):
            _, rows, low = factors(sk[pl.ds(base, 8), c : c + CHUNK])
            hi, lo = split(jnp.concatenate(monomials(rows, low), axis=0))
            value = cols[c : c + CHUNK, :]
            p = dot(hi, value) + dot(lo, value)
            acc = p if acc is None else acc + p
        tab = acc[:, :128] + acc[:, 128:]
        if len(refs) > 3:
            tab = tab + refs[0][0, g]
        tab_ref[0, g] = tab


def read_kernel(
    hashes, groups, inner, q_ref, v_ref, tab_ref, proj_ref, taps_ref, num_ref, conv_ref, cnt_ref, sq,
):
    head = pl.program_id(0)
    width = q_ref.shape[2]
    block = width // (groups * inner)
    sq[...] = signs_of(q_ref[0], proj_ref[...])
    num_ref[0] = jnp.zeros(num_ref.shape[1:], F32)
    natural = reorder(v_ref[0], inner, groups, block)
    conv = jnp.zeros(natural.shape, F32)
    for j in range(CONV):
        conv = conv + shifted(natural, j - HALF) * taps_ref[head, j]
    conv_ref[0] = reorder(conv, groups, inner, block)

    @pl.loop(0, hashes)
    def _(g):
        base = pl.multiple_of(g * 8, 8)
        flat = (tab_ref[0, g] * (1.0 / BUCKETS)).T[:ROWS]
        cnt_ref[0, pl.ds(g, 1), :] = flat[64:65]
        ext = jnp.concatenate(split(flat), axis=0)
        for c in range(0, width, CHUNK):
            _, rows, low = factors(sq[pl.ds(base, 8), c : c + CHUNK])
            hi, lo = split(jnp.concatenate(monomials(rows, low), axis=0))
            p = dot(ext, hi)
            num_ref[0, :, c : c + CHUNK] += p[:ROWS] + p[ROWS:] + dot(ext[:ROWS], lo)


def bwd_kernel(
    hashes, groups, inner, head, part, qkv_hbm, valid_ref, proj_ref, num_hbm, da_hbm, tab_hbm, taps_ref, *refs
):
    before_hbm = refs[0] if part else None
    out_hbm, dt_ref, q_ref, k_ref, v_ref, num_ref, da_ref, tab_ref, before_ref, sq, sk, gq, gk, cols, xq, xk, dv, sems = refs[
        1 if part else 0 :
    ]
    heads, width = num_hbm.shape[0], q_ref.shape[2]
    block = width // (groups * inner)
    sources = (
        qkv_hbm.at[head], qkv_hbm.at[heads + head], qkv_hbm.at[2 * heads + head], num_hbm.at[head], da_hbm.at[head],
        tab_hbm.at[head, part * hashes : (part + 1) * hashes],
    )
    targets = (q_ref, k_ref, v_ref, num_ref, da_ref, tab_ref)
    copies = [
        pltpu.make_async_copy(source, target.at[0], sems.at[i])
        for i, (source, target) in enumerate(zip(sources, targets))
    ]
    if part:
        copies.append(pltpu.make_async_copy(before_hbm, before_ref, sems.at[6]))
    for copy in copies:
        copy.start()
    copies[0].wait()
    sq[...] = signs_of(q_ref[0], proj_ref[...])
    copies[1].wait()
    sk[...] = signs_of(k_ref[0], proj_ref[...])
    for copy in copies[2:5]:
        copy.wait()
    da = da_ref[0]
    v = v_ref[0]
    inv = 1.0 / (num_ref[0, 64:65, :] + HASH_COUNT)
    dn = da * inv
    dd = -jnp.sum(dn * num_ref[0, :64, :], axis=0, keepdims=True) * inv
    cols[...] = columns(dn, dd)
    xq[...] = stacked(dn, dd)
    xk[...] = stacked(v, valid_ref[...])
    dv[...] = jnp.zeros(dv.shape, F32)
    copies[5].wait()

    @pl.loop(0, hashes)
    def _(g):
        base = pl.multiple_of(g * 8, 8)
        tabs = beside(tab_ref[0, g] * (1.0 / BUCKETS))
        acc = None
        for c in range(0, width, CHUNK):
            s8 = sq[pl.ds(base, 8), c : c + CHUNK]
            r, rows, low = factors(s8)
            phi = monomials(rows, low)
            hi, lo = split(jnp.concatenate(phi, axis=0))
            value = cols[c : c + CHUNK, :]
            p = dot(hi, value) + dot(lo, value)
            acc = p if acc is None else acc + p
            d = dot(tabs, xq[:, c : c + CHUNK])
            gq[pl.ds(base, 8), c : c + CHUNK] = sign_grad(r, rows, low, phi, d) * (2.0 - 2.0 * s8 * s8)
        tab = (acc[:, :128] + acc[:, 128:]) * (1.0 / BUCKETS)
        ext = halves(tab)
        tabs = beside(tab)
        for c in range(0, width, CHUNK):
            s8 = sk[pl.ds(base, 8), c : c + CHUNK]
            r, rows, low = factors(s8)
            phi = monomials(rows, low)
            hi, lo = split(jnp.concatenate(phi, axis=0))
            p = dot(ext, hi)
            dv[:, c : c + CHUNK] += p[:ROWS] + p[ROWS:] + dot(ext[:ROWS], lo)
            d = dot(tabs, xk[:, c : c + CHUNK])
            gk[pl.ds(base, 8), c : c + CHUNK] = sign_grad(r, rows, low, phi, d) * (2.0 - 2.0 * s8 * s8)

    back = proj_ref[...].T
    if part:
        copies[6].wait()
    copies = [
        pltpu.make_async_copy(source.at[0], out_hbm.at[64 * i : 64 * i + 64], sems.at[i])
        for i, source in enumerate((q_ref, k_ref, v_ref))
    ]
    total = dv[:64, :]
    if part == 0:
        natural = reorder(v, inner, groups, block)
        grad = reorder(da, inner, groups, block)
        conv = jnp.zeros(natural.shape, F32)
        for j in range(CONV):
            conv = conv + shifted(grad, HALF - j) * taps_ref[0, j]
            moved = grad * shifted(natural, j - HALF)
            dt_ref[j : j + 1, :] = jnp.sum(moved, axis=0, keepdims=True)
        total = total + reorder(conv, groups, inner, block)
    total = total * valid_ref[...]
    v_ref[0] = total + before_ref[128:, :] if part else total
    copies[2].start()
    for i, (u_ref, g_ref) in enumerate(((q_ref, gq), (k_ref, gk))):
        u = u_ref[0]
        scale = norm_scale(u)
        g = dot3(back, g_ref[...])
        inside = g - u * (scale * scale * jnp.mean(g * u, axis=0, keepdims=True))
        grad = (scale * 0.125) * inside
        u_ref[0] = grad + before_ref[64 * i : 64 * i + 64, :] if part else grad
        copies[i].start()
    for copy in copies:
        copy.wait()


def one(*shape, at=0):
    return pl.BlockSpec((1,) + shape, lambda h: (h + at,) + (0,) * len(shape))


def same(*shape):
    return pl.BlockSpec(shape, lambda h: (0,) * len(shape))


SMEM = pl.BlockSpec(memory_space=pltpu.SMEM)


def fill(qkv, valid, proj, tab):
    heads, width = qkv.shape[0] // 3, qkv.shape[2]
    hashes = proj.shape[0] // 8
    parts = 4
    ins = [qkv, qkv, valid, proj] + [tab] * (tab is not None)

    def rows(at):
        return pl.BlockSpec((1, 64, width), lambda h, p: (h + at, 0, 0))

    table = pl.BlockSpec((1, hashes // parts, BUCKETS, 128), lambda h, p: (h, p, 0, 0))
    specs = [
        rows(heads), rows(2 * heads), pl.BlockSpec((1, width), lambda h, p: (0, 0)),
        pl.BlockSpec(proj.shape, lambda h, p: (0, 0)), table,
    ]
    return pl.pallas_call(
        fill_kernel,
        grid=(heads, parts),
        in_specs=specs[: len(ins)],
        out_specs=table,
        out_shape=jax.ShapeDtypeStruct((heads, hashes, BUCKETS, 128), F32),
        scratch_shapes=[pltpu.VMEM((hashes * 8, width), F32), pltpu.VMEM((width, 256), BF)],
        compiler_params=pltpu.CompilerParams(vmem_limit_bytes=OUTER_VMEM),
        cost_estimate=pl.CostEstimate(flops=0, bytes_accessed=0, transcendentals=0),
        name="fill",
    )(*ins)


def read(qkv, tab, proj, taps, groups, inner):
    heads, width = qkv.shape[0] // 3, qkv.shape[2]
    hashes = proj.shape[0] // 8
    return pl.pallas_call(
        functools.partial(read_kernel, hashes, groups, inner),
        grid=(heads,),
        in_specs=[
            one(64, width), one(64, width, at=2 * heads), one(hashes, BUCKETS, 128), same(*proj.shape), SMEM,
        ],
        out_specs=[one(ROWS, width), one(64, width), one(hashes, BUCKETS)],
        out_shape=[
            jax.ShapeDtypeStruct((heads, ROWS, width), F32),
            jax.ShapeDtypeStruct((heads, 64, width), F32),
            jax.ShapeDtypeStruct((heads, hashes, BUCKETS), F32),
        ],
        scratch_shapes=[pltpu.VMEM((hashes * 8, width), F32)],
        compiler_params=pltpu.CompilerParams(vmem_limit_bytes=VMEM_BYTES),
        cost_estimate=pl.CostEstimate(flops=0, bytes_accessed=0, transcendentals=0),
        name="read",
    )(qkv, qkv, tab, proj, taps)


def attend_back(head, part, parts, qkv, valid, proj, num, d_attn, tab, taps, before, groups, inner):
    width = qkv.shape[2]
    hashes = proj.shape[0] // 8 // parts
    hbm = pl.BlockSpec(memory_space=pltpu.HBM)
    rows = pltpu.VMEM((1, 64, width), F32)
    ins = [qkv, valid, proj, num, d_attn, tab, taps] + [before] * (part > 0)
    specs = [hbm, same(1, width), pl.BlockSpec((hashes * 8, 64), lambda _: (part, 0)), hbm, hbm, hbm, SMEM, hbm]
    return pl.pallas_call(
        functools.partial(bwd_kernel, hashes, groups, inner, head, part),
        grid=(1,),
        in_specs=specs[: len(ins)],
        out_specs=[hbm, same(16, width)],
        out_shape=[jax.ShapeDtypeStruct((192, width), F32), jax.ShapeDtypeStruct((16, width), F32)],
        scratch_shapes=[rows] * 3
        + [pltpu.VMEM((1, ROWS, width), F32), rows, pltpu.VMEM((1, hashes, BUCKETS, 128), F32)]
        + [pltpu.VMEM((192, width), F32)]
        + [pltpu.VMEM((hashes * 8, width), F32)] * 4
        + [pltpu.VMEM((width, 256), BF)]
        + [pltpu.VMEM((256, width), BF)] * 2
        + [pltpu.VMEM((ROWS, width), F32), pltpu.SemaphoreType.DMA((7,))],
        compiler_params=pltpu.CompilerParams(vmem_limit_bytes=BACK_VMEM),
        cost_estimate=pl.CostEstimate(flops=0, bytes_accessed=0, transcendentals=0),
        name="attend_back",
    )(*ins)


def weights_kernel(count, c_ref, *refs):
    parts, (hi_ref, lo_ref, w_ref, sum_ref, mine_ref, full_ref) = refs[:count], refs[count:]
    full = parts[0][...]
    for part in parts[1:]:
        full = full + part[...]
    full_ref[...] = full
    fh, fl = split(full)
    w_ref[...] = dot(fh, hi_ref[...]) + dot(fl, hi_ref[...]) + dot(fh, lo_ref[...])
    sum_ref[...] = jnp.broadcast_to(jnp.sum(full, axis=1, keepdims=True), sum_ref.shape)
    size = mine_ref.shape[1]
    mine_ref[...] = full_ref[:, pl.ds(pl.multiple_of(c_ref[0] * size, 128), size)]


def weights_of(parts, x_parts, c):
    features, tokens = parts[0].shape
    ins = [*parts, *x_parts]
    vmem = pl.BlockSpec(memory_space=pltpu.VMEM)
    return pl.pallas_call(
        functools.partial(weights_kernel, len(parts)),
        in_specs=[SMEM] + [vmem] * len(ins),
        out_specs=[vmem] * 3,
        out_shape=[
            jax.ShapeDtypeStruct((features, x_parts[0].shape[1]), F32),
            jax.ShapeDtypeStruct((features, 128), F32),
            jax.ShapeDtypeStruct((features, tokens // len(parts)), F32),
        ],
        scratch_shapes=[pltpu.VMEM((features, tokens), F32)],
        compiler_params=pltpu.CompilerParams(vmem_limit_bytes=VMEM_BYTES),
        cost_estimate=pl.CostEstimate(flops=0, bytes_accessed=0, transcendentals=0),
        name="weights_of",
    )(c.reshape(1), *ins)


def copy_kernel(x_ref, o_ref):
    o_ref[...] = x_ref[...]


def widened(x, columns):
    size = MODEL_WIDTH
    return pl.pallas_call(
        copy_kernel,
        grid=(columns // size, 2),
        in_specs=[pl.BlockSpec((size // 2, size), lambda j, i: (j * 2 + i, 0))],
        out_specs=pl.BlockSpec((size // 2, size), lambda j, i: (i, j)),
        out_shape=jax.ShapeDtypeStruct((size, columns), x.dtype),
        compiler_params=pltpu.CompilerParams(vmem_limit_bytes=OUTER_VMEM),
        cost_estimate=pl.CostEstimate(flops=0, bytes_accessed=0, transcendentals=0),
        name="widened",
    )(x)


def rejoin_kernel(c_ref, *refs):
    count = len(refs) - 3
    rows = refs[-1].shape[0]
    for s in range(count):

        @pl.when(pl.program_id(0) == s)
        def _():
            for i in range(3):
                refs[count + i][...] = refs[s][i, :rows]


def rejoined(parts, rows, c):
    count, columns = len(parts), parts[0].shape[2]
    out = pl.BlockSpec((rows, columns), lambda s, c_ref: (lax.rem(c_ref[0] + count - s, count), 0))
    return pl.pallas_call(
        rejoin_kernel,
        grid_spec=pltpu.PrefetchScalarGridSpec(
            num_scalar_prefetch=1,
            grid=(count,),
            in_specs=[pl.BlockSpec(t.shape, lambda *_: (0, 0, 0)) for t in parts],
            out_specs=[out] * 3,
        ),
        out_shape=[jax.ShapeDtypeStruct((count * rows, columns), F32)] * 3,
        compiler_params=pltpu.CompilerParams(vmem_limit_bytes=VMEM_BYTES),
        cost_estimate=pl.CostEstimate(flops=0, bytes_accessed=0, transcendentals=0),
        name="rejoined",
    )(c.reshape(1), *parts)


def copied(x):
    rows, columns = x.shape
    block = rows // 8
    spec = pl.BlockSpec((block, columns), lambda i: (i, 0))
    return pl.pallas_call(
        copy_kernel,
        grid=(8,),
        in_specs=[spec],
        out_specs=spec,
        out_shape=jax.ShapeDtypeStruct(x.shape, x.dtype),
        compiler_params=pltpu.CompilerParams(vmem_limit_bytes=OUTER_VMEM),
        cost_estimate=pl.CostEstimate(flops=0, bytes_accessed=0, transcendentals=0),
        name="copied",
    )(x)


def outer_kernel(inner, c_ref, a_ref, b_ref, *refs):
    *out_refs, whole = refs
    items, rows = out_refs[0].shape[:2]
    ah, al = split(a_ref[...])
    bh, bl = split(b_ref[...])
    dims = (((0,), (0,)), ((), ()))
    whole[...] = (
        lax.dot_general(ah, bh, dims, preferred_element_type=F32)
        + lax.dot_general(al, bh, dims, preferred_element_type=F32)
        + lax.dot_general(ah, bl, dims, preferred_element_type=F32)
    )
    for s, out_ref in enumerate(out_refs):
        start = lax.rem(c_ref[0] + s, inner) * rows
        for i in range(items):
            out_ref[i] = whole[pl.ds(pl.multiple_of(i * inner * rows + start, 8), rows), :]


def outer_blocks(a, b, items, inner, c):
    tokens, wide = a.shape
    block, columns = wide // items, b.shape[1]
    each = 1 if block % 128 == 0 else items
    width = min(columns, MODEL_WIDTH)
    return pl.pallas_call(
        functools.partial(outer_kernel, inner),
        grid=(items // each, columns // width),
        in_specs=[
            SMEM,
            pl.BlockSpec((tokens, each * block), lambda i, j: (0, i)),
            pl.BlockSpec((tokens, width), lambda i, j: (0, j)),
        ],
        out_specs=[pl.BlockSpec((each, block // inner, width), lambda i, j: (i, 0, j))] * inner,
        out_shape=[jax.ShapeDtypeStruct((items, block // inner, columns), F32)] * inner,
        scratch_shapes=[pltpu.VMEM((each * block, width), F32)],
        compiler_params=pltpu.CompilerParams(vmem_limit_bytes=OUTER_VMEM),
        cost_estimate=pl.CostEstimate(flops=0, bytes_accessed=0, transcendentals=0),
        name="outer_blocks",
    )(c.reshape(1), a, b)


def rows_kernel(
    inner, c_ref, first_ref, hidden_ref, attn_ref, pre_ref, second_ref, d_first_ref, n1_ref, n2_ref, grad_ref, *out_refs
):
    s, item, k = (pl.program_id(i) for i in range(3))
    block = (item * inner + lax.rem(c_ref[0] + s, inner)) * pl.num_programs(2) + k
    size = out_refs[0].shape[0]
    each = MODEL_WIDTH // size
    ups = hidden_ref.shape[1] // MODEL_WIDTH * each

    def product(a, b, dims):
        ah, al = split(a)
        bh, bl = split(b)
        return sum(
            lax.dot_general(x, y, (dims, ((), ())), preferred_element_type=F32)
            for x, y in ((ah, bh), (al, bh), (ah, bl))
        )

    def put(value):
        for i, out_ref in enumerate(out_refs):

            @pl.when(s == i)
            def _():
                out_ref[...] = value

    @pl.when(block < ups)
    def _():
        at = pl.multiple_of(lax.rem(block, each) * size, size)
        to = pl.multiple_of(lax.div(block, each) * MODEL_WIDTH, MODEL_WIDTH)
        put(product(first_ref[:, pl.ds(at, size)], hidden_ref[:, pl.ds(to, MODEL_WIDTH)], ((0,), (0,))))

    @pl.when((block >= ups) & (block < ups + each))
    def _():
        at = pl.multiple_of((block - ups) * size, size)
        put(product(attn_ref[pl.ds(at, size), :], pre_ref[...], ((1,), (0,))))

    @pl.when(block == ups + each)
    def _():
        def down(t):
            return jnp.sum(t, axis=0, keepdims=True)

        rows = [
            down(pre_ref[...]), down(d_first_ref[...] * n1_ref[...]), down(d_first_ref[...]), down(second_ref[...]),
            down(grad_ref[...] * n2_ref[...]), down(grad_ref[...]),
        ]
        wide = hidden_ref.shape[1]
        rows += [down(hidden_ref[:, j : j + MODEL_WIDTH]) for j in range(0, wide, MODEL_WIDTH)]
        rows.append(jnp.zeros((size - len(rows), MODEL_WIDTH), F32))
        put(jnp.concatenate(rows))

    @pl.when(block > ups + each)
    def _():
        put(jnp.zeros((size, MODEL_WIDTH), F32))


def outer_rows(first, d_hidden, attn_t, d_pre, others, items, inner, c):
    rows = (d_hidden.shape[1] + MODEL_WIDTH + 256) // (items * inner)
    size = 256 if rows % 256 == 0 else 128
    blocks = rows // size

    def place(i):
        last = items * blocks - 1

        def index(s, item, k, _):
            at = item * blocks + k
            return jnp.where(s == i, at, jnp.where(s > i, last, 0)), 0

        return pl.BlockSpec((size, MODEL_WIDTH), index)

    ins = [first, d_hidden, attn_t, d_pre, *others]
    shape = jax.ShapeDtypeStruct((items * rows, MODEL_WIDTH), F32)
    parts = pl.pallas_call(
        functools.partial(rows_kernel, inner),
        grid_spec=pltpu.PrefetchScalarGridSpec(
            num_scalar_prefetch=1,
            grid=(inner, items, blocks),
            in_specs=[pl.BlockSpec(t.shape, lambda *_: (0, 0)) for t in ins],
            out_specs=[place(i) for i in range(inner)],
        ),
        out_shape=[shape] * inner,
        compiler_params=pltpu.CompilerParams(vmem_limit_bytes=VMEM_BYTES),
        cost_estimate=pl.CostEstimate(flops=0, bytes_accessed=0, transcendentals=0),
        name="outer_rows",
    )(c.reshape(1), *ins)
    return [t.reshape(items, -1, MODEL_WIDTH) for t in parts]


AXES = ("item", "z", "core")
ITEM, Z, C = range(3)


class Grid:
    def __init__(self, sizes):
        self.sizes = sizes
        self.place = tuple(lax.axis_index(name) for name in AXES)
        self.found = []

    def send(self, x, axis, target):
        sizes = self.sizes
        pairs = []
        for source in itertools.product(*(range(n) for n in sizes)):
            to = target(source[axis])
            if to is None:
                continue
            there = source[:axis] + (to,) + source[axis + 1 :]
            flat = [functools.reduce(lambda t, ni: t * ni[0] + ni[1], zip(sizes, p), 0) for p in (source, there)]
            pairs.append(tuple(flat))
        return lax.ppermute(x, AXES, pairs)

    def ordered(self, parts, axis):
        count, own = len(parts), self.place[axis]
        if count == 1:
            return parts
        if count == 2:
            swap = own == 1
            return [jnp.where(swap, parts[1], parts[0]), jnp.where(swap, parts[0], parts[1])]
        whole = jnp.stack(parts)
        return [lax.dynamic_index_in_dim(whole, (own - s) % count, 0, keepdims=False) for s in range(count)]

    def offer(self, x, axis):
        count = self.sizes[axis]
        return [x] + [self.send(x, axis, lambda i: (i + s) % count) for s in range(1, count)]

    def collect(self, parts, axis, dim=None):
        parts = self.ordered(parts, axis)
        return parts if dim is None else jnp.concatenate(parts, axis=dim)

    def spread(self, x, axis):
        return jnp.stack(self.collect(self.offer(x, axis), axis))

    def deal(self, x, axis, dim=0):
        count, own = self.sizes[axis], self.place[axis]
        size = x.shape[dim] // count
        parts = [x]
        for s in range(1, count):
            block = lax.dynamic_slice_in_dim(x, (own + s) % count * size, size, dim)
            parts.append(self.send(block, axis, lambda i: (i + s) % count))
        return parts

    def own_block(self, x, axis, dim):
        size = x.shape[dim] // self.sizes[axis]
        return lax.dynamic_slice_in_dim(x, self.place[axis] * size, size, dim)

    def add(self, parts, axis, dim=0):
        total = self.own_block(parts[0], axis, dim)
        for part in parts[1:]:
            total = total + part
        return total

    def take(self, parts, axis, dim=0):
        return self.ordered([self.own_block(parts[0], axis, dim)] + parts[1:], axis)

    def arrivals(self, axis):
        count = self.sizes[axis]
        return [
            sorted((s, d) for s in range(1, count) for d in (-1, 1) if 0 <= i + d * s < count) for i in range(count)
        ]

    def step_on(self, up, down, axis, step):
        count = self.sizes[axis]
        up = self.send(up, axis, lambda i: i + 1 if step - 1 <= i < count - 1 else None)
        down = self.send(down, axis, lambda i: i - 1 if 0 < i <= count - step else None)
        return up, down

    def arrived(self, came, axis, k):
        own, result = self.place[axis], None
        for i, moves in enumerate(self.arrivals(axis)):
            step, way = moves[k - 1]
            candidate = came[step][(way + 1) // 2]
            result = candidate if result is None else jnp.where(own == i, candidate, result)
        return result

    def places(self, axis):
        count, own = self.sizes[axis], self.place[axis]
        j = lax.iota(jnp.int32, count)
        s = jnp.abs(j - own)
        before = jnp.minimum(s - 1, own) + jnp.minimum(s - 1, count - 1 - own)
        both = ((j > own) & (own >= s)).astype(jnp.int32)
        places = jnp.where(j == own, 0, before + both + 1)
        return [places[i] for i in range(count)]

    def by_index(self, parts, places):
        whole = jnp.stack(parts)
        return [lax.dynamic_index_in_dim(whole, place, 0, keepdims=False) for place in places]


    def dealing(self, x, axis, dim=0):
        count, own = self.sizes[axis], self.place[axis]
        size = x.shape[dim] // count
        blocks = [lax.dynamic_slice_in_dim(x, (own + s) % count * size, size, dim) for s in range(count)]
        return (yield from self.moving(axis, blocks))

    def moving(self, axis, blocks):
        yield axis, blocks
        return (yield)

    def applying(self, function, x):
        yield function, [x]
        return (yield)

    def move(self, axis, blocks_of):
        count = self.sizes[axis]
        result = [[blocks[0]] for blocks in blocks_of]
        for s in range(1, count):
            out = [blocks[s] if len(blocks) > 1 else blocks[0] for blocks in blocks_of]
            if len(out) == 1:
                result[0].append(self.send(out[0], axis, lambda i: (i + s) % count))
                continue
            lane = functools.reduce(math.gcd, (t.shape[1] for t in out))
            lanes = [[t[:, k : k + lane] for k in range(0, t.shape[1], lane)] for t in out]
            whole = self.send(jnp.concatenate(sum(lanes, [])), axis, lambda i: (i + s) % count)
            row = 0
            for t, into in zip(out, result):
                rows, wide = t.shape[0], t.shape[1] // lane
                pieces = [whole[row + k * rows : row + (k + 1) * rows] for k in range(wide)]
                into.append(jnp.concatenate(pieces, axis=1))
                row += rows * wide
        return result

    def reduce(self, blocks):
        blocks = yield blocks
        x = sum((yield from self.moving(C, blocks)))
        scatter = functools.partial(lax.psum_scatter, axis_name="item", scatter_dimension=0, tiled=True)
        x = (yield from self.applying(scatter, x))[0][0]
        x = sum((yield from self.dealing(x, Z)))
        x = self.collect((yield from self.moving(Z, [x])), Z, 0)
        gather = functools.partial(lax.all_gather, axis_name=("item", "core"), axis=0, tiled=True)
        return (yield from self.applying(gather, x))

    def head(self, d_part, x_parts):
        d_part = yield d_part
        parts = yield from self.moving(C, [d_part])
        self.found.append(weights_of(parts, x_parts, self.place[C]))

    def home(self, mine):
        mine = yield mine
        return (yield from self.dealing(mine, Z, 1))

    def tail(self, d_w):
        d_w = yield d_w
        feats = d_w.shape[1] // 3
        x = sum((yield from self.dealing(d_w, ITEM)))
        x = self.collect((yield from self.moving(Z, [x])), Z)
        x = [jnp.concatenate([t[:, i * feats : (i + 1) * feats] for t in x], axis=1) for i in range(3)]
        x = yield from self.moving(ITEM, [jnp.stack(x)])
        return (yield from self.moving(C, [self.collect(x, ITEM, 1)]))


class Steps:
    def __init__(self, grid):
        self.grid, self.live, self.state, self.done = grid, {}, {}, {}

    def add(self, name, sequence):
        self.live[name], self.state[name] = sequence, next(sequence)

    def advance(self, states):
        ready = {}
        for name, state in states.items():
            try:
                ready[name] = self.live[name].send(state)
            except StopIteration as end:
                self.done[name] = end.value
                del self.live[name], self.state[name]
        return {name: how for name, (how, _) in ready.items()}, {name: blocks for name, (_, blocks) in ready.items()}

    def carry(self, hows, blocks):
        came = {}
        for axis in (C, Z, ITEM):
            names = [name for name, how in hows.items() if how == axis]
            alike = [name for name in names if axis == Z and blocks[name][0].shape[1] % 128 == 0 and name != "up"]
            groups = [alike] * bool(alike) + [[name] for name in names if name not in alike]
            for group in groups:
                came.update(zip(group, self.grid.move(axis, [blocks[name] for name in group])))
        for name, how in hows.items():
            if callable(how):
                came[name] = how(blocks[name][0])
                came[name] = [came[name]] if how.func is lax.psum_scatter else came[name]
            next(self.live[name])
            self.state[name] = came[name]

    def start(self, name):
        self.carry(*self.advance({name: self.state[name]}))

    def stage(self, names, held=(), beside=()):
        names = [name for name in names if name in self.live]
        states, held = lax.optimization_barrier(({name: self.state[name] for name in names}, held))
        hows, blocks = self.advance(states)
        blocks, beside = lax.optimization_barrier((blocks, beside))
        self.carry(hows, blocks)
        return held, beside


def normalize(x):
    centered = x - jnp.mean(x, axis=-1, keepdims=True)
    scale = lax.rsqrt(jnp.mean(centered * centered, axis=-1, keepdims=True) + 1e-05)
    return centered * scale, scale


def normalize_back(grad, normed, scale):
    mean = jnp.mean(grad, axis=-1, keepdims=True)
    along = jnp.mean(grad * normed, axis=-1, keepdims=True)
    return scale * (grad - mean - normed * along)


def dense(x, attn_t, out_grad, w_out, b_out, gain_one, bias_one, w_up, b_up, w_down, b_down, gain_two, bias_two):
    n1, scale1 = normalize(x + by_weight(attn_t, w_out, 0, 0) + b_out)
    first = n1 * gain_one + bias_one
    hidden = by_weight(first, w_up, 1, 0) + b_up
    cdf = 0.5 + 0.5 * lax.erf(hidden * math.sqrt(0.5))
    inner = hidden * cdf
    n2, scale2 = normalize(first + by_weight(inner, w_down, 1, 0) + b_down)
    output = n2 * gain_two + bias_two
    d_second = normalize_back(out_grad * gain_two, n2, scale2)
    slope = cdf + hidden * (jnp.exp(-0.5 * hidden * hidden) * (1.0 / math.sqrt(2.0 * math.pi)))
    d_hidden = by_weight(d_second, w_down, 1, 1) * slope
    d_first = d_second + by_weight(d_hidden, w_up, 1, 1)
    d_pre = normalize_back(d_first * gain_one, n1, scale1)
    d_hi, d_lo = parts_of(d_pre)
    d_attn_t = contract(w_out, d_hi, 1, 1) + contract(w_out, d_lo, 1, 1)
    return output, d_attn_t, (d_second, first, d_hidden, attn_t, d_pre, d_first, n1, n2, out_grad, inner)


def hadamard():
    index = lax.iota(jnp.int32, BUCKETS)
    both = lax.population_count(index[:, None] & index[None, :])
    return jnp.where((both & 1) == 0, 1.0, -1.0).astype(BF)


def per_device(
    sizes, inputs, lengths, pad_mask, hash_proj, w_query, b_query, w_key, b_key, w_value, b_value, conv_taps,
    w_out, b_out, gain_one, bias_one, w_up, b_up, w_down, b_down, gain_two, bias_two, out_grad,
):
    grid = Grid(sizes)
    items, groups, inner = sizes
    count = groups * inner
    _, z, c = grid.place
    heads = HEAD_COUNT // groups
    feats = heads * HEAD_SIZE
    own_hashes = HASH_COUNT // count
    hashes = own_hashes * groups
    tokens = inputs.shape[1]
    width = count * tokens
    x = inputs[0]

    position = (z * inner + c) * tokens + lax.iota(jnp.int32, tokens)
    valid = ((position < lengths[0]) & (pad_mask[0] == 1)).astype(F32)
    mask_rows = jnp.pad(valid.reshape(1, tokens), ((0, 7), (0, MODEL_WIDTH - tokens)))

    def head_columns(w):
        return lax.dynamic_slice_in_dim(w, z * feats, feats, axis=w.ndim - 1)

    w_qkv = jnp.concatenate([head_columns(w) for w in (w_query, w_key, w_value)], axis=1)
    b_qkv = jnp.concatenate([head_columns(b) for b in (b_query, b_key, b_value)])

    is_value = lax.iota(jnp.int32, 3 * feats)[:, None] >= 2 * feats

    def project(rows):
        hi, lo = parts_of(rows[:tokens])
        here = rows[tokens : tokens + 1, :tokens]
        products = contract(w_qkv, hi, 0, 1) + contract(w_qkv, lo, 0, 1) + b_qkv[:, None]
        products = jnp.where(is_value, products * here, products)
        products = jnp.concatenate([products, jnp.broadcast_to(here, (8, tokens))])
        return grid.collect(grid.offer(products, C), C, 1)

    proj = lax.dynamic_index_in_dim(
        hash_proj.reshape(HEAD_SIZE, groups, inner, own_hashes * HASH_BITS), c, 2, keepdims=False
    )
    proj = proj.reshape(HEAD_SIZE, hashes * HASH_BITS).T
    taps = lax.dynamic_slice_in_dim(conv_taps, z * heads, heads, axis=0)
    up = down = jnp.concatenate([x, mask_rows])
    came, lines, chunks, tab = [(up, down)], [up], [], None
    places = grid.places(Z)
    for k in range(groups):
        if k:
            up, down, tab, chunks, places, taps = lax.optimization_barrier((up, down, tab, chunks, places, taps))
            came.append((up, down))
            lines.append(grid.arrived(came, Z, k))
        if k < groups - 1:
            up, down = grid.step_on(up, down, Z, k + 1)
        chunk = project(lines[-1])
        chunks.append(chunk)
        per_head = chunk[: 3 * feats].reshape(3 * heads, HEAD_SIZE, -1)
        tab = fill(per_head, chunk[3 * feats : 3 * feats + 1], proj, tab)
    tab, chunks = lax.optimization_barrier((tab, chunks))
    chunks = grid.by_index(chunks, places)
    chunks = jnp.concatenate(
        [t[:, i * tokens : (i + 1) * tokens] for i in range(inner) for t in chunks], axis=1
    )
    qkv, valid = chunks[: 3 * feats].reshape(3 * heads, HEAD_SIZE, width), chunks[3 * feats : 3 * feats + 1]

    num_part, conv, subsets = read(qkv, tab, proj, taps, groups, inner)
    half = groups * tokens
    own_num = grid.add(grid.deal(num_part, C, dim=2), C, dim=2)
    lines, own_num = lax.optimization_barrier((lines, own_num))
    x_line = jnp.stack(grid.by_index(lines, places))
    num = grid.collect(grid.offer(own_num, C), C, 2)
    own_conv = lax.dynamic_slice_in_dim(conv, c * half, half, 2)
    attn = own_num[:, :HEAD_SIZE] / (own_num[:, HEAD_SIZE : HEAD_SIZE + 1] + HASH_COUNT) + own_conv
    attn = grid.deal(attn.reshape(feats, half), Z, dim=1)

    rows = MODEL_WIDTH // inner
    x_line = x_line[:, :tokens].reshape(half, MODEL_WIDTH)
    x_half = parts_of(jnp.concatenate(grid.take(grid.deal(x_line, C, dim=1), C, dim=1)))
    attn, x_half, num = lax.optimization_barrier((attn, x_half, num))
    attn_t = jnp.concatenate(grid.take(attn, Z, dim=1))

    subsets = subsets.reshape(heads * hashes, BUCKETS)
    sub_hi, sub_rest = parts_of(subsets)
    sub_mid, sub_lo = parts_of(subsets - sub_hi.astype(F32))
    signs = hadamard()
    own_counts = contract(sub_hi, signs, 1, 0) + contract(sub_mid, signs, 1, 0) + contract(sub_lo, signs, 1, 0)
    own_counts = own_counts.reshape(heads, groups, own_hashes, BUCKETS).transpose(1, 0, 2, 3)

    steps = Steps(grid)
    output, d_attn_t, held = dense(
        x, attn_t, out_grad[0],
        w_out, b_out, gain_one, bias_one, w_up, b_up, w_down, b_down, gain_two, bias_two,
    )
    d_line = jnp.concatenate([d_attn_t.reshape(groups, feats, tokens), own_counts.reshape(groups, -1, tokens)], axis=1)
    d_line = [lax.dynamic_index_in_dim(d_line, (z + s) % groups, 0, keepdims=False) for s in range(groups)]
    d_line, held = lax.optimization_barrier((d_line, held))
    d_line = [d_line[0]] + [grid.send(t, Z, lambda i: (i + s) % groups) for s, t in enumerate(d_line[1:], 1)]
    d_second, first, d_hidden, attn_t, d_pre, d_first, n1, n2, cotangent, inside = held
    steps.add("down", grid.reduce(outer_blocks(inside, d_second, items, inner, c)))
    steps.start("down")
    others = (d_second, d_first, n1, n2, cotangent)
    rest = outer_rows(first, d_hidden, attn_t, d_pre, others, items, inner, c)
    d_line, rest, steps.state["down"] = lax.optimization_barrier((d_line, rest, steps.state["down"]))
    steps.add("rest", grid.reduce(rest))
    steps.start("rest")

    def enter(d_line):
        d_line = grid.ordered(d_line, Z)
        own = jnp.concatenate([t[:feats] for t in d_line], axis=1)
        counts = jnp.stack([t[feats:] for t in d_line]).reshape(HEAD_COUNT, own_hashes, BUCKETS)
        return grid.collect(grid.offer(own, C), C, 1).reshape(heads, HEAD_SIZE, width), counts

    d_all, counts = enter(d_line)

    plan = [["down"], ["rest"], ["down", "head0"], ["down"], ["down", "rest", "head0", "head1"], ["rest"]]
    first_c = jnp.where(c == 0, 1.0, 0.0)

    def staged(names, held=(), beside=()):
        before, count = grid.found, len(grid.found)
        (held, ready), beside = steps.stage(names, (held, before), beside)
        grid.found = ready + before[count:]
        return held, beside

    found, last = [], ()
    for call in range(heads * BACK_PARTS):
        head, part = call // BACK_PARTS, call % BACK_PARTS
        if call < len(plan):
            last, d_all = staged(plan[call], last, d_all)
            if call:
                found.append(last)
        own_taps = taps[head : head + 1] * first_c
        before = last[0] if part else None
        last = attend_back(head, part, BACK_PARTS, qkv, valid, proj, num, d_all, tab, own_taps, before, groups, inner)
        if part == BACK_PARTS - 1:
            steps.add(f"head{head}", grid.head(last[0], x_half))
    found.append(last)
    d_t = [jnp.sum(found[head * BACK_PARTS][1][:CONV], axis=1) * first_c for head in range(heads)]
    last_head = f"head{heads - 1}"
    others = [name for name in steps.live if name.startswith("head") and name != last_head]
    staged(others + [last_head, "rest"])
    staged([last_head])
    steps.add("home", grid.home(jnp.concatenate([t[2] for t in grid.found])))
    d_w = jnp.stack([t[0].reshape(3, HEAD_SIZE, -1) for t in grid.found], axis=1).reshape(3 * feats, -1).T
    d_b = jnp.stack([t[1][:, 0].reshape(3, HEAD_SIZE) for t in grid.found], axis=1).reshape(-1)
    d_t = jnp.pad(jnp.concatenate(d_t), (0, 3 * feats - heads * CONV))
    rows = MODEL_WIDTH // inner
    below = jnp.pad(jnp.stack([d_b, d_t]), ((0, EXTRA - 2), (0, 0)))
    steps.add("tail", grid.tail(jnp.concatenate([d_w, below])))
    def input_part(blocks, first_head):
        count = blocks[0].shape[0] // (3 * HEAD_SIZE)
        total = 0.0
        for i, w in enumerate((w_query, w_key, w_value)):
            spans = [slice((k * 3 + i) * HEAD_SIZE, (k * 3 + i + 1) * HEAD_SIZE) for k in range(count)]
            d = jnp.concatenate([t[span] for t in blocks for span in spans])
            w = w.reshape(MODEL_WIDTH, groups, heads, HEAD_SIZE)[:, :, first_head : first_head + count]
            total = total + by_weight(d, w.reshape(MODEL_WIDTH, -1), 0, 1)
        return total

    steps.stage(["tail"])
    steps.stage(["tail"])
    steps.stage(["tail", "down", "home"])
    d_down = copied(steps.done["down"])
    steps.advance({"rest": steps.state["rest"]})
    rest, wide = steps.done["rest"], w_up.shape[1]
    d_up = widened(rest, wide)
    d_out, last_rows = rest[wide : wide + MODEL_WIDTH], rest[wide + MODEL_WIDTH :]
    (d_down, d_up, d_out, last_rows), _ = steps.stage(["tail", "home"], (d_down, d_up, d_out, last_rows))
    d_x = held[4] + input_part(grid.ordered(steps.done["home"], Z), 0)
    d_x, _ = steps.stage(["tail"], d_x)
    tail = steps.done["tail"]
    weights = rejoined(tail, rows, c)
    below = tail[0][:, rows:]
    for s in range(1, inner):
        below = jnp.where(c == s, tail[s][:, rows:], below)
    d_b = below[:, 0]
    d_conv_taps = below[0, 1].reshape(groups, feats)[:, : heads * CONV].reshape(HEAD_COUNT, CONV)
    names = ("b_out", "gain_one", "bias_one", "b_down", "gain_two", "bias_two")
    vectors = dict(zip(names, last_rows))
    vectors["b_up"] = last_rows[len(names) : len(names) + wide // MODEL_WIDTH].reshape(-1)

    result = []
    for i in range(3):
        result += [weights[i], d_b[i]]
    result += [
        d_conv_taps, d_out, vectors["b_out"], vectors["gain_one"], vectors["bias_one"], d_up, vectors["b_up"],
        d_down, vectors["b_down"], vectors["gain_two"], vectors["bias_two"],
    ]
    return (output[None], d_x[None], counts[None], *result)


def solution(mesh):
    items, count = mesh.shape["item"], mesh.shape["seq"]
    groups = math.gcd(HEAD_COUNT, count)
    sizes = (items, groups, count // groups)
    seq = ("z", "core")
    tokens = P("item", seq, None)
    in_specs = (tokens, P("item"), P("item", seq)) + (P(),) * 18 + (tokens,)
    out_specs = (tokens, tokens, P("item", None, seq, None)) + (P(),) * 17
    return jax.shard_map(
        functools.partial(per_device, sizes),
        mesh=Mesh(mesh.devices.reshape(sizes), AXES),
        in_specs=in_specs,
        out_specs=out_specs,
        check_vma=False,
    )
```
